256 devices in a mesh: dp: 16 (over x, y_hi, core), tensor: 16 (over y_lo, z).
Axes of the slice: x: 4, y: 4 (y_hi: 2, y_lo: 2; y = y_hi * 2 + y_lo), z: 8, core: 2. Of those that a mesh axis runs over, the one named last changes fastest.
Arguments:
- learner_layer_inputs: bfloat16 [49152, 16384], P('dp', 'tensor'), may hold values from -6 to 6
- trainer_lookup_content_adjoint: bfloat16 [49152, 2048], P('dp', 'tensor'), may hold values from -6 to 6
- frozen_weight: bfloat16 [16384, 2048], P('tensor'), may hold values from -0.046875 to 0.046875
- shrink_matrices: float32 [16384, 128], P('tensor'), may hold values from -0.046875 to 0.046875
- expand_matrices: float32 [64, 2048], P(None, 'tensor'), may hold values from -0.3 to 0.3
- decode_hidden_states: bfloat16 [4096, 16384], P('dp', 'tensor'), may hold values from -6 to 6
- rms_norm_gain: float32 [16384], P('tensor'), may hold values from 0.1 to 1.9
Outputs:
- new_keys_values: float32 [2048, 4096], P('tensor', 'dp')
The draws below stay inside these ranges and needn't reach their ends.
All inputs are finite; a program needn't handle non-finite values.
Results may differ from the reference program's by a relative error of at most 0.0041.
Values sent between devices are 32-bit elements; how exact they have to be, the bound alone decides.
A program may use at most 64 MiB of HBM per device.

```python
import jax
import jax.numpy as jnp
from jax import lax

EMBED_DIMENSION = 16384
ATTN_HEAD_DIMS = 1024
ADAPT_INNER_DIM = 64
TOKENS = 49152
DECODE = 4096


def steps_of(rng, dims, pieces, low, largest):
    def one(position, blocks):
        heights = jax.random.uniform(jax.random.fold_in(jax.random.fold_in(rng, 6), position), (blocks,), jnp.float32, low / len(pieces), largest / len(pieces))
        return jnp.repeat(jnp.exp(heights), dims[position] // blocks).reshape((-1,) + (1,) * (len(dims) - position - 1))

    factor_of = one(*pieces[0])
    for cut in pieces[1:]:
        factor_of = factor_of * one(*cut)
    return factor_of


def normal_values(own_key, extent, spread, bound, split=(), kind=jnp.bfloat16):
    gain = steps_of(own_key, extent, split, -0.22, 0.18) if split else 1.0
    entries = jax.random.normal(own_key, extent, jnp.float32) * spread * gain
    return jnp.minimum(jnp.maximum(entries, -bound), bound).astype(kind)


def setup_inputs(seed: int = 0) -> dict:
    keys = jax.random.split(jax.random.key(seed), 8)
    learner_layer_inputs = normal_values(keys[0], (TOKENS, EMBED_DIMENSION), 1.0, 6.0, ((0, 16), (1, 16)))
    trainer_lookup_content_adjoint = normal_values(keys[1], (TOKENS, 2 * ATTN_HEAD_DIMS), 1.0, 6.0, ((0, 16), (1, 16)))
    frozen_weight = normal_values(keys[2], (EMBED_DIMENSION, 2 * ATTN_HEAD_DIMS), EMBED_DIMENSION ** -0.5, 0.046875, ((0, 16),))
    shrink_matrices = normal_values(keys[3], (EMBED_DIMENSION, 2 * ADAPT_INNER_DIM), EMBED_DIMENSION ** -0.5, 0.046875, ((0, 16),), jnp.float32)
    expand_matrices = normal_values(keys[4], (ADAPT_INNER_DIM, 2 * ATTN_HEAD_DIMS), 0.05, 0.3, ((1, 16),), jnp.float32)
    decode_hidden_states = normal_values(keys[5], (DECODE, EMBED_DIMENSION), 1.0, 6.0, ((0, 16), (1, 16)))
    rms_norm_gain = jnp.clip(1.0 + 0.18 * jax.random.normal(keys[6], (EMBED_DIMENSION,), jnp.float32), 0.1, 1.9)
    return {"learner_layer_inputs": learner_layer_inputs, "trainer_lookup_content_adjoint": trainer_lookup_content_adjoint, "frozen_weight": frozen_weight, "shrink_matrices": shrink_matrices, "expand_matrices": expand_matrices, "decode_hidden_states": decode_hidden_states, "rms_norm_gain": rms_norm_gain}


delta_multiplier = 2.0
learning_rate = 4.0
clip_limit = 1.0

def token_axis_summation(left, right):
    return lax.dot_general(left, right, (((0,), (0,)), ((), ())), preferred_element_type=jnp.float32)

def reference(learner_layer_inputs, trainer_lookup_content_adjoint, frozen_weight, shrink_matrices, expand_matrices, decode_hidden_states, rms_norm_gain):
    down_factor_cast = shrink_matrices.astype(jnp.bfloat16)
    up_factor_cast = expand_matrices.astype(jnp.bfloat16)
    mapped_result = (delta_multiplier * jnp.dot(learner_layer_inputs, down_factor_cast, preferred_element_type=jnp.float32)).astype(jnp.bfloat16)
    back_key = jnp.dot(trainer_lookup_content_adjoint[:, :ATTN_HEAD_DIMS], up_factor_cast[:, :ATTN_HEAD_DIMS].T, preferred_element_type=jnp.float32)
    back_value = jnp.dot(trainer_lookup_content_adjoint[:, ATTN_HEAD_DIMS:], up_factor_cast[:, ATTN_HEAD_DIMS:].T, preferred_element_type=jnp.float32)
    gradient_held = (delta_multiplier * jnp.concatenate([back_key, back_value], axis=1)).astype(jnp.bfloat16)
    down_gradient = token_axis_summation(learner_layer_inputs, gradient_held)
    expand_derivative = jnp.concatenate([token_axis_summation(mapped_result[:, :ADAPT_INNER_DIM], trainer_lookup_content_adjoint[:, :ATTN_HEAD_DIMS]), token_axis_summation(mapped_result[:, ADAPT_INNER_DIM:], trainer_lookup_content_adjoint[:, ATTN_HEAD_DIMS:])], axis=1)
    total = jnp.sum(down_gradient * down_gradient) + jnp.sum(expand_derivative * expand_derivative)
    factor_matrix = jnp.minimum(1.0, clip_limit / (jnp.sqrt(total) + 1e-06))
    revised_shrink_matrix = shrink_matrices - learning_rate * factor_matrix * down_gradient
    revised_expand_matrix = expand_matrices - learning_rate * factor_matrix * expand_derivative
    attention_lookup_thin = jnp.dot(revised_shrink_matrix[:, :ADAPT_INNER_DIM], revised_expand_matrix[:, :ATTN_HEAD_DIMS], precision=lax.Precision.HIGHEST)
    content_thin_product = jnp.dot(revised_shrink_matrix[:, ADAPT_INNER_DIM:], revised_expand_matrix[:, ATTN_HEAD_DIMS:], precision=lax.Precision.HIGHEST)
    merged_weight = (frozen_weight.astype(jnp.float32) + delta_multiplier * jnp.concatenate([attention_lookup_thin, content_thin_product], axis=1)).astype(jnp.bfloat16)
    widened = decode_hidden_states.astype(jnp.float32)
    meansq = lax.optimization_barrier(jnp.mean(widened * widened, axis=1))
    normed = (widened * lax.rsqrt(meansq + 1e-05)[:, None] * rms_norm_gain[None, :]).astype(jnp.bfloat16)
    result = lax.dot_general(merged_weight, normed, (((0,), (1,)), ((), ())), preferred_element_type=jnp.float32)
    return result
```

```python
import functools

import jax
import jax.numpy as jnp
from jax import lax
from jax.experimental import pallas as pl
from jax.experimental.pallas import tpu as pltpu
from jax.sharding import PartitionSpec as P

MESH = pl.DeviceIdType.MESH
F32 = jnp.float32
BF16 = jnp.bfloat16

EMBED_DIMENSION = 16384
delta_multiplier = 2.0
learning_rate = 4.0
clip_limit = 1.0

Z = 8
T = 16
E = 8
CH = 192
HALF = 1536


def rc(src, dst, ss, rs, dev):
    return pltpu.make_async_remote_copy(
        src_ref=src, dst_ref=dst, send_sem=ss, recv_sem=rs, device_id=dev, device_id_type=MESH
    )


def low_lanes(rows):
    return lax.broadcasted_iota(jnp.int32, (rows, 128), 1) < 64


def swap(v):
    return pltpu.roll(v, 64, 1)


def dot(a, b):
    return jnp.dot(a, b, preferred_element_type=F32)


def dot_nt(a, b):
    return lax.dot_general(a, b, (((1,), (1,)), ((), ())), preferred_element_type=F32)


def dot_tn(a, b):
    return lax.dot_general(a, b, (((0,), (0,)), ((), ())), preferred_element_type=F32)


def split(v):
    hi = v.astype(BF16)
    return hi, (v - hi.astype(F32)).astype(BF16)


class RingReduce:
    def __init__(self, own, buf, ss, rs, z, dev):
        self.own, self.buf, self.ss, self.rs, self.z, self.dev = own, buf, ss, rs, z, dev

    def chunk(self, d, far):
        return lax.rem(self.z + (far if d == 0 else Z - far), Z)

    def copy(self, d, h, s):
        first = 1 if d == h else 2
        if s == first:
            src = self.own(self.chunk(d, 5 - s), h)
        else:
            src = self.buf.at[d, s - 2, h]
        return rc(src, self.buf.at[d, s - 1, h], self.ss.at[d, h, s - 1], self.rs.at[d, h, s - 1], self.dev(d))

    def begin(self, first):
        for d in range(2):
            h = d if first == 1 else 1 - d
            self.copy(d, h, first).start()

    def step(self, s):
        for same in (True, False):
            if s == 1 and not same:
                continue
            for d in range(2):
                h = d if same else 1 - d
                self.copy(d, h, s).wait_recv()
                if s < 4:
                    self.buf[d, s - 1, h] += self.own(self.chunk(d, 4 - s), h)[...]
                    self.copy(d, h, s + 1).start()

    def result(self, h):
        return self.own(self.z, h)[...] + (self.buf[0, 3, h] + self.buf[1, 3, h])

    def drain(self):
        for d in range(2):
            for h in range(2):
                for s in range(1 if d == h else 2, 5):
                    self.copy(d, h, s).wait_send()


class RingGather:
    def __init__(self, arr, ss, rs, z, dev):
        self.arr, self.ss, self.rs, self.z, self.dev = arr, ss, rs, z, dev

    def copy(self, d, p, s):
        k = lax.rem(self.z + (Z - (s - 1) if d == 0 else s - 1), Z)
        ref = self.arr.at[k, p]
        return rc(ref, ref, self.ss.at[d, p, s - 1], self.rs.at[d, p, s - 1], self.dev(d))

    def begin(self):
        for p in range(2):
            for d in range(2):
                self.copy(d, p, 1).start()

    def step(self, s):
        for p in range(2):
            for d in range(2):
                last = 4 if d == p else 3
                if s <= last:
                    self.copy(d, p, s).wait_recv()
                    if s + 1 <= last:
                        self.copy(d, p, s + 1).start()

    def drain(self):
        for d in range(2):
            for p in range(2):
                for s in range(1, (4 if d == p else 3) + 1):
                    self.copy(d, p, s).wait_send()


def kernel(
    x_hbm, a_hbm, w_hbm, d_hbm, u_hbm, h_hbm, gain_hbm, o_ref,
    xv, av, wv, dv, uv, hv, gv, db, ub,
    bm, br, bag, pm, pt, py, pr, pag, om, oy, orr,
    gt, gc, gr, gf, gu, gur, guc, guf, rows, norms, normed, base,
    q0, q0r, q0a, qg, qgr, qga,
    ld, xs, s4, r4, y_s, y_r, t_s, t_r, z_s, z_r, e_s, e_r, c_s, c_r,
):
    dpi = lax.axis_index("dp")
    t = lax.axis_index("tensor")
    e, c = dpi // 2, lax.rem(dpi, 2)
    y, z = t // Z, lax.rem(t, Z)
    zdev = (dpi, y * Z + lax.rem(z + 1, Z)), (dpi, y * Z + lax.rem(z + Z - 1, Z))
    ydev = (dpi, (1 - y) * Z + z)
    cdev = (e * 2 + 1 - c, t)

    def ring(d):
        return zdev[d]

    def tdev(k):
        return (dpi, k)

    def edev(k):
        return (k * 2 + c, t)

    def order(j):
        far = 4 - (j + 1) // 2
        return lax.rem(z + (1 - 2 * lax.rem(j + 1, 2)) * far + Z, Z)

    def loop(n, body):
        def step(i, carry):
            body(i)
            return carry

        lax.fori_loop(0, n, step, 0)

    def local(src, dst, i):
        return pltpu.make_async_copy(src, dst, ld.at[i])

    l_u, l_a, l_d = local(u_hbm, uv, 0), local(a_hbm, av, 1), local(d_hbm, dv, 2)
    l_h, l_g, l_w = local(h_hbm, hv, 3), local(gain_hbm, gv, 4), local(w_hbm, wv, 5)

    def tok(k, second):
        return pl.ds(pl.multiple_of(k * CH + second * HALF, CH), CH)

    def xload(j, second):
        sl = tok(order(j), second)
        return pltpu.make_async_copy(x_hbm.at[sl], xv.at[sl], xs.at[j, second])

    l_u.start()
    l_a.start()
    l_d.start()

    @functools.partial(loop, Z)
    def _(j):
        xload(j, 0).start()
        xload(j, 1).start()

    l_h.start()
    l_g.start()
    l_w.start()

    barrier = pltpu.get_barrier_semaphore()

    def hello(dev):
        pl.semaphore_signal(barrier, inc=1, device_id=dev, device_id_type=MESH)

    hello(cdev)
    loop(T - 1, lambda i: hello(tdev(lax.rem(t + 1 + i, T))))
    loop(E - 1, lambda i: hello(edev(lax.rem(e + 1 + i, E))))

    l_u.wait()
    l_a.wait()
    ub[...] = uv[...].astype(BF16)
    blank = jnp.zeros((64, 128), BF16)

    @functools.partial(loop, Z)
    def _(k):
        u1 = jnp.concatenate([ub[...], blank], axis=0)
        u2 = jnp.concatenate([blank, ub[...]], axis=0)
        v = dot_nt(av[tok(k, 0), :], u1) + dot_nt(av[tok(k, 1), :], u2)
        bm[k] = v.reshape(2, CH // 2, 128)

    pl.semaphore_wait(barrier, T - 1 + E - 1 + 1)

    b_rs = RingReduce(lambda k, h: bm.at[k, h], br, s4.at[0], r4.at[0], z, ring)
    b_ag = RingGather(bag, s4.at[1], r4.at[1], z, ring)
    p_rs = RingReduce(lambda k, h: pm.at[k, h], pr, s4.at[2], r4.at[2], z, ring)
    p_ag = RingGather(pag, s4.at[3], r4.at[3], z, ring)
    o_rs = RingReduce(lambda k, h: om.at[y * Z + k, h], orr, s4.at[4], r4.at[4], z, ring)
    b_rs.begin(1)
    b_rs.begin(2)

    def p_y(j):
        k = order(j)
        return rc(pt.at[k], py.at[k], y_s.at[0, j], y_r.at[0, j], ydev)

    def o_y(j):
        k = order(j)
        return rc(om.at[(1 - y) * Z + k], oy.at[k], y_s.at[1, j], y_r.at[1, j], ydev)

    b_y = rc(bag.at[z, y], bag.at[z, y], y_s.at[2, 0], y_r.at[2, 0], ydev)
    b_y_in = rc(bag.at[z, 1 - y], bag.at[z, 1 - y], y_s.at[2, 0], y_r.at[2, 0], ydev)

    def p_add(j):
        p_y(j).wait_recv()
        k = order(j)
        pm[k] += py[k]

    def o_add(j):
        o_y(j).wait_recv()
        k = order(j)
        om[y * Z + k] += oy[k]

    l_d.wait()
    dd = dv[...]
    db[...] = jnp.where(y == 0, dd, swap(dd)).astype(BF16)

    @functools.partial(loop, Z)
    def _(j):
        k = order(j)
        xload(j, 0).wait()
        xload(j, 1).wait()
        pa = dot(xv[tok(k, 0), :], db[...])
        pb = dot(xv[tok(k, 1), :], db[...])
        low = low_lanes(CH)
        pm[k] = jnp.where(low, pa, swap(pb)).reshape(2, CH // 2, 128)
        pt[k] = jnp.where(low, swap(pa), pb).reshape(2, CH // 2, 128)

        @pl.when(j < 4)
        def _():
            p_y(j).start()

    def t_copy(n, src, dst, k):
        return rc(src, dst, t_s.at[n, k], t_r.at[n, t], tdev(k))

    def t_send(n, src, dst):
        loop(T - 1, lambda i: t_copy(n, src(lax.rem(t + 1 + i, T)), dst, lax.rem(t + 1 + i, T)).start())

    def t_recv(n, like, dst):
        def body(i):
            k = lax.rem(t + 1 + i, T)
            rc(like, dst.at[k], t_s.at[n, k], t_r.at[n, k], tdev(k)).wait_recv()

        loop(T - 1, body)

    def t_drain(n, src, dst):
        loop(T - 1, lambda i: t_copy(n, src(lax.rem(t + 1 + i, T)), dst, lax.rem(t + 1 + i, T)).wait_send())

    def z_copy(n, arr, i):
        k = lax.rem(z + 1 + i, Z)
        return rc(arr.at[z], arr.at[z], z_s.at[n, k], z_r.at[n, z], tdev(y * Z + k))

    def z_send(n, arr):
        loop(Z - 1, lambda i: z_copy(n, arr, i).start())

    def z_recv(n, arr):
        def body(i):
            k = lax.rem(z + 1 + i, Z)
            rc(arr.at[k], arr.at[k], z_s.at[n, k], z_r.at[n, k], tdev(y * Z + k)).wait_recv()

        loop(Z - 1, body)

    def e_copy(n, src, dst, k):
        return rc(src, dst, e_s.at[n, k], e_r.at[n, e], edev(k))

    def e_each(body):
        loop(E - 1, lambda i: body(lax.rem(e + 1 + i, E)))

    def pack(v, n):
        low = low_lanes(n)
        a, b = v[:n], v[n:]
        return jnp.where(low, a, swap(b)), jnp.where(low, swap(a), b)

    l_h.wait()
    l_g.wait()
    hf = hv[...].astype(F32)
    sq = jnp.sum(hf * hf, axis=1, keepdims=True)
    rows[t] = jnp.transpose(jnp.broadcast_to(sq, (256, 128)))[:8]
    t_send(0, lambda k: rows.at[t], rows.at[t])

    b_rs.step(1)
    p_add(0)
    p_rs.begin(1)
    b_rs.step(2)
    p_add(1)
    p_add(2)
    p_rs.begin(2)
    b_rs.step(3)
    p_rs.step(1)
    b_rs.step(4)
    for h in range(2):
        bag[z, y, h * 96 : (h + 1) * 96] = b_rs.result(h)
    b_y.start()
    loop(4, lambda j: p_y(j + 4).start())

    t_recv(0, rows.at[t], rows)
    mean = jnp.sum(rows[...], axis=0) / EMBED_DIMENSION
    scale = lax.rsqrt(mean + 1e-05)
    scale = jnp.transpose(jnp.broadcast_to(scale[:1], (128, 256)))
    for i in range(8):
        sl = slice(i * 128, (i + 1) * 128)
        normed[:, sl] = (hv[:, sl].astype(F32) * scale * gv[:, sl]).astype(BF16)

    b_y_in.wait_recv()
    b_ag.begin()

    l_w.wait()

    def out_pair(i):
        v = dot(normed[...], wv[:, pl.ds(pl.multiple_of(i * 256, 256), 256)])
        om[2 * i] = v[:, :128].reshape(2, 128, 128)
        om[2 * i + 1] = v[:, 128:].reshape(2, 128, 128)

    loop(4, lambda i: out_pair((1 - y) * 4 + i))
    loop(Z, lambda j: o_y(j).start())

    p_add(3)
    p_add(4)
    p_rs.step(2)

    def grad(k):
        kc, vc = bag[k, 0], bag[k, 1]
        low = low_lanes(CH)
        ba = jnp.where(low, kc, swap(vc)) * delta_multiplier
        bb = jnp.where(low, swap(kc), vc) * delta_multiplier
        v = dot_tn(ba.astype(BF16), xv[tok(k, 0), :]) + dot_tn(bb.astype(BF16), xv[tok(k, 1), :])
        return v.reshape(16, 8, 1024)

    gt[...] = grad(z)
    b_ag.step(1)
    loop(4, lambda i: out_pair(y * 4 + i))
    p_add(5)
    p_add(6)
    p_rs.step(3)
    loop(2, lambda i: gt.__setitem__(Ellipsis, gt[...] + grad(lax.rem(z + 1 + i * (Z - 2), Z))))
    b_ag.step(2)

    dhi, dlo = split(dv[...])
    qk, qv = pack(dot(normed[...], dhi) + dot(normed[...], dlo), 128)
    q0[0:8] = qk.reshape(8, 16, 128)
    q0[8:16] = qv.reshape(8, 16, 128)
    q0r[t] = q0[t]
    t_send(1, lambda k: q0.at[k], q0r.at[t])

    loop(2, lambda i: gt.__setitem__(Ellipsis, gt[...] + grad(lax.rem(z + 2 + i * (Z - 4), Z))))
    p_add(7)
    p_rs.step(4)
    for h in range(2):
        pag[z, h] = p_rs.result(h)
    b_ag.step(3)
    p_ag.begin()
    loop(2, lambda i: gt.__setitem__(Ellipsis, gt[...] + grad(lax.rem(z + 3 + i * (Z - 6), Z))))
    b_ag.step(4)
    gt[...] = gt[...] + grad(lax.rem(z + 4, Z))

    mine = pl.ds(pl.multiple_of(c * 8, 8), 8)
    other = pl.ds(pl.multiple_of((1 - c) * 8, 8), 8)
    g_c = rc(gt.at[other], gc, c_s.at[0], c_r.at[0], cdev)
    g_c.start()
    p_ag.step(1)
    g_c.wait_recv()
    gt[mine] += gc[...]
    gr[e] = gt[c * 8 + e]
    e_each(lambda k: e_copy(0, gt.at[c * 8 + k], gr.at[e], k).start())
    p_ag.step(2)

    t_recv(1, q0.at[t], q0r)
    q0a[z] = jnp.sum(q0r[...], axis=0)
    z_send(0, q0a)

    o_add(0)
    o_rs.begin(1)
    e_each(lambda k: rc(gt.at[c * 8 + k], gr.at[k], e_s.at[0, k], e_r.at[0, k], edev(k)).wait_recv())
    gf[c * 8 + e] = jnp.sum(gr[...], axis=0)
    e_each(lambda k: e_copy(1, gf.at[c * 8 + e], gf.at[c * 8 + e], k).start())

    def g_share(k):
        ref = gf.at[c * 8 + k]
        return rc(ref, ref, c_s.at[2 + k], c_r.at[2 + k], cdev)

    g_share(e).start()
    p_ag.step(3)
    o_add(1)
    o_add(2)
    o_rs.begin(2)
    p_ag.step(4)

    gu[...] = jnp.zeros_like(gu)

    @functools.partial(loop, Z)
    def _(k):
        pc = (pag[k].reshape(CH, 128) * delta_multiplier).astype(BF16)
        va = dot_tn(pc, av[tok(k, 0), :])
        vb = dot_tn(pc, av[tok(k, 1), :])
        gu[...] += (va[:64] + vb[64:]).reshape(8, 8, 128)

    gur[e] = gu[e]
    e_each(lambda k: e_copy(2, gu.at[k], gur.at[e], k).start())

    def g_pass(k):
        ref = gf.at[c * 8 + k]
        rc(ref, ref, e_s.at[1, k], e_r.at[1, k], edev(k)).wait_recv()
        g_share(k).start()

    e_each(g_pass)

    def g_share_in(k):
        ref = gf.at[(1 - c) * 8 + k]
        rc(ref, ref, c_s.at[2 + k], c_r.at[2 + k], cdev).wait_recv()

    loop(E, g_share_in)
    ghi, glo = split(gf[...].reshape(128, 1024))
    qk, qv = pack(dot_nt(normed[...], ghi) + dot_nt(normed[...], glo), 128)
    qg[0:8] = qk.reshape(8, 16, 128)
    qg[8:16] = qv.reshape(8, 16, 128)
    qgr[t] = qg[t]
    t_send(2, lambda k: qg.at[k], qgr.at[t])

    o_rs.step(1)
    o_add(3)
    o_add(4)
    e_each(lambda k: rc(gu.at[k], gur.at[k], e_s.at[2, k], e_r.at[2, k], edev(k)).wait_recv())
    guc[c] = jnp.sum(gur[...], axis=0)
    gu_c = rc(guc.at[c], guc.at[c], c_s.at[1], c_r.at[1], cdev)
    gu_c.start()
    o_rs.step(2)
    rc(guc.at[1 - c], guc.at[1 - c], c_s.at[1], c_r.at[1], cdev).wait_recv()
    guf[e] = guc[0] + guc[1]
    e_each(lambda k: e_copy(3, guf.at[e], guf.at[e], k).start())
    o_add(5)
    o_add(6)

    t_recv(2, qg.at[t], qgr)
    qga[z] = jnp.sum(qgr[...], axis=0)
    z_send(1, qga)
    o_rs.step(3)

    e_each(lambda k: rc(guf.at[k], guf.at[k], e_s.at[3, k], e_r.at[3, k], edev(k)).wait_recv())
    g2 = jnp.sum(gf[...] * gf[...], axis=0)
    tile = jnp.sum(guf[...] * guf[...], axis=0)
    for i in range(8):
        tile = tile + g2[:, i * 128 : (i + 1) * 128]
    norms[t] = tile
    t_send(3, lambda k: norms.at[t], norms.at[t])

    o_add(7)
    o_rs.step(4)
    for h in range(2):
        base[h] = o_rs.result(h)
    z_recv(0, q0a)
    z_recv(1, qga)
    t_recv(3, norms.at[t], norms)
    total = jnp.sum(jnp.sum(norms[...], axis=0), keepdims=True)
    factor = jnp.minimum(1.0, clip_limit / (jnp.sqrt(total) + 1e-06))
    q = q0a[...].reshape(128, 128) - learning_rate * factor * qga[...].reshape(128, 128)
    up = uv[...] - learning_rate * factor * guf[...].reshape(64, 128)
    zero = jnp.zeros_like(up)
    for h in range(2):
        wide = jnp.concatenate([up, zero] if h == 0 else [zero, up], axis=0)
        v = jnp.dot(q, wide, precision=lax.Precision.HIGHEST, preferred_element_type=F32)
        o_ref[:, h * 128 : (h + 1) * 128] = jnp.transpose(base[h] + delta_multiplier * v)

    b_rs.drain()
    b_ag.drain()
    p_rs.drain()
    p_ag.drain()
    o_rs.drain()
    b_y.wait_send()

    @functools.partial(loop, Z)
    def _(j):
        p_y(j).wait_send()
        o_y(j).wait_send()
        g_share(j).wait_send()

    t_drain(0, lambda k: rows.at[t], rows.at[t])
    t_drain(1, lambda k: q0.at[k], q0r.at[t])
    t_drain(2, lambda k: qg.at[k], qgr.at[t])
    t_drain(3, lambda k: norms.at[t], norms.at[t])

    @functools.partial(loop, Z - 1)
    def _(i):
        z_copy(0, q0a, i).wait_send()
        z_copy(1, qga, i).wait_send()

    def e_drain(k):
        e_copy(0, gt.at[c * 8 + k], gr.at[e], k).wait_send()
        e_copy(1, gf.at[c * 8 + e], gf.at[c * 8 + e], k).wait_send()
        e_copy(2, gu.at[k], gur.at[e], k).wait_send()
        e_copy(3, guf.at[e], guf.at[e], k).wait_send()

    e_each(e_drain)
    g_c.wait_send()
    gu_c.wait_send()


def shards(x, a, w, d, u, hidden, gain):
    V = pltpu.VMEM
    dma = pltpu.SemaphoreType.DMA
    part = (8, 2, 96, 128)
    scratch = [
        V((3072, 1024), BF16), V((3072, 128), BF16), V((1024, 2048), BF16), V((1024, 128), F32),
        V((64, 128), F32), V((256, 1024), BF16), V((1, 1024), F32), V((1024, 128), BF16), V((64, 128), BF16),
        V(part, F32), V((2, 4, 2, 96, 128), F32), V((8, 2, 192, 128), F32),
        V(part, F32), V(part, F32), V(part, F32), V((2, 4, 2, 96, 128), F32), V(part, F32),
        V((16, 2, 128, 128), F32), V((8, 2, 128, 128), F32), V((2, 4, 2, 128, 128), F32),
        V((16, 8, 1024), F32), V((8, 8, 1024), F32), V((8, 8, 1024), F32), V((16, 8, 1024), F32),
        V((8, 8, 128), F32), V((8, 8, 128), F32), V((2, 8, 128), F32), V((8, 8, 128), F32),
        V((16, 8, 256), F32), V((16, 8, 128), F32), V((256, 1024), BF16), V((2, 128, 128), F32),
        V((16, 16, 128), F32), V((16, 16, 128), F32), V((8, 16, 128), F32),
        V((16, 16, 128), F32), V((16, 16, 128), F32), V((8, 16, 128), F32),
        dma((6,)), dma((8, 2)), dma((5, 2, 2, 4)), dma((5, 2, 2, 4)), dma((3, 8)), dma((3, 8)),
        dma((4, 16)), dma((4, 16)), dma((2, 8)), dma((2, 8)), dma((4, 8)), dma((4, 8)), dma((10,)), dma((10,)),
    ]
    return pl.pallas_call(
        kernel,
        out_shape=jax.ShapeDtypeStruct((128, 256), F32),
        in_specs=[pl.BlockSpec(memory_space=pl.ANY)] * 7,
        out_specs=pl.BlockSpec(memory_space=pltpu.VMEM),
        scratch_shapes=scratch,
        compiler_params=pltpu.CompilerParams(
            collective_id=0, has_side_effects=True, vmem_limit_bytes=56 << 20
        ),
    )(x, a, w, d, u, hidden, gain.reshape(1, 1024))


def solution(mesh):
    placed = (
        P("dp", "tensor"),
        P("dp", "tensor"),
        P("tensor", None),
        P("tensor", None),
        P(None, "tensor"),
        P("dp", "tensor"),
        P("tensor"),
    )
    return jax.shard_map(
        shards, mesh=mesh, in_specs=placed, out_specs=P("tensor", "dp"), check_vma=False
    )
```

```python
import functools

import jax
import jax.numpy as jnp
from jax import lax
from jax.experimental import pallas as pl
from jax.experimental.pallas import tpu as pltpu
from jax.sharding import PartitionSpec as P

MESH = pl.DeviceIdType.MESH
F32 = jnp.float32
BF16 = jnp.bfloat16

EMBED_DIMENSION = 16384
delta_multiplier = 2.0
learning_rate = 4.0
clip_limit = 1.0

Z = 8
T = 16
E = 8
CH = 192


def rc(src, dst, ss, rs, dev):
    return pltpu.make_async_remote_copy(
        src_ref=src, dst_ref=dst, send_sem=ss, recv_sem=rs, device_id=dev, device_id_type=MESH
    )


def low_lanes(rows):
    return lax.broadcasted_iota(jnp.int32, (rows, 128), 1) < 64


def swap(v):
    return pltpu.roll(v, 64, 1)


def dot(a, b):
    return jnp.dot(a, b, preferred_element_type=F32)


def dot_nt(a, b):
    return lax.dot_general(a, b, (((1,), (1,)), ((), ())), preferred_element_type=F32)


def dot_tn(a, b):
    return lax.dot_general(a, b, (((0,), (0,)), ((), ())), preferred_element_type=F32)


def split(v):
    hi = v.astype(BF16)
    return hi, (v - hi.astype(F32)).astype(BF16)


class RingReduce:
    def __init__(self, own, buf, ss, rs, z, dev):
        self.own, self.buf, self.ss, self.rs, self.z, self.dev = own, buf, ss, rs, z, dev

    def chunk(self, d, far):
        return lax.rem(self.z + (far if d == 0 else Z - far), Z)

    def slot(self, d, h, s):
        return d * 7 + (s - 1 if d == h else 4 + s - 2)

    def copy(self, d, h, s):
        first = 1 if d == h else 2
        if s == first:
            src = self.own(self.chunk(d, 5 - s), h)
        else:
            src = self.buf.at[self.slot(d, h, s - 1)]
        i = self.slot(d, h, s)
        return rc(src, self.buf.at[i], self.ss, self.rs.at[i], self.dev(d))

    def begin(self, first):
        for d in range(2):
            h = d if first == 1 else 1 - d
            self.copy(d, h, first).start()

    def step(self, s):
        for same in (True, False):
            if s == 1 and not same:
                continue
            for d in range(2):
                h = d if same else 1 - d
                self.copy(d, h, s).wait_recv()
                if s < 4:
                    self.buf[self.slot(d, h, s)] += self.own(self.chunk(d, 4 - s), h)[...]
                    self.copy(d, h, s + 1).start()

    def result(self, h):
        return self.own(self.z, h)[...] + (self.buf[self.slot(0, h, 4)] + self.buf[self.slot(1, h, 4)])

    def drain(self):
        rc(self.buf, self.buf, self.ss, self.rs.at[0], self.dev(0)).wait_send()


class RingGather:
    def __init__(self, arr, ss, rs, z, dev):
        self.arr, self.ss, self.rs, self.z, self.dev = arr, ss, rs, z, dev

    def copy(self, d, p, s):
        k = lax.rem(self.z + (Z - (s - 1) if d == 0 else s - 1), Z)
        ref = self.arr.at[k, p]
        i = d * 7 + (s - 1 if d == p else 4 + s - 1)
        return rc(ref, ref, self.ss, self.rs.at[i], self.dev(d))

    def begin(self, p):
        for d in range(2):
            self.copy(d, p, 1).start()

    def step(self, p, s):
        for d in (p, 1 - p):
            last = 4 if d == p else 3
            if s <= last:
                self.copy(d, p, s).wait_recv()
                if s + 1 <= last:
                    self.copy(d, p, s + 1).start()

    def drain(self):
        all_sent = self.arr.at[0:7]
        rc(all_sent, all_sent, self.ss, self.rs.at[0], self.dev(0)).wait_send()


def kernel(
    x_hbm, a_hbm, w_hbm, d_hbm, u_hbm, h_hbm, gain_hbm, o_ref,
    xv, av, wv, dv, uv, hv, gv, db, ub,
    bm, br, bag, pm, pt, py, pr, pag, om, oy, orr,
    gt, gc, gr, gf, gu, guc, gur, guf, rows, norms, normed, base,
    q0a, qg, qgr, qga,
    ld, xs, ring_r, py_r, oy_r, y_r, t_r, z_r, e_r, c_r, sent,
):
    dpi = lax.axis_index("dp")
    t = lax.axis_index("tensor")
    e, c = dpi // 2, lax.rem(dpi, 2)
    y, z = t // Z, lax.rem(t, Z)
    zdev = (dpi, y * Z + lax.rem(z + 1, Z)), (dpi, y * Z + lax.rem(z + Z - 1, Z))
    ydev = (dpi, (1 - y) * Z + z)
    cdev = (e * 2 + 1 - c, t)

    def ring(d):
        return zdev[d]

    def tdev(k):
        return (dpi, k)

    def edev(k):
        return (k * 2 + c, t)

    def order(j):
        far = 4 - (j + 1) // 2
        return lax.rem(z + (1 - 2 * lax.rem(j + 1, 2)) * far + Z, Z)

    def loop(n, body, first=0):
        def step(i, carry):
            body(i)
            return carry

        lax.fori_loop(first, n, step, 0)

    def both(far, body):
        if far in (0, 4):
            body(lax.rem(z + far, Z))
        else:
            loop(2, lambda i: body(lax.rem(z + far + i * (Z - 2 * far), Z)))

    def local(src, dst, i):
        return pltpu.make_async_copy(src, dst, ld.at[i])

    l_u, l_a, l_d = local(u_hbm, uv, 0), local(a_hbm, av, 1), local(d_hbm, dv, 2)
    l_h, l_g, l_w = local(h_hbm, hv, 3), local(gain_hbm, gv, 4), local(w_hbm, wv, 5)

    def xload(j):
        k = order(j)
        return pltpu.make_async_copy(x_hbm.at[:, k], xv.at[:, k], xs.at[j])

    l_u.start()
    l_a.start()
    l_d.start()
    loop(Z, lambda j: xload(j).start())
    l_h.start()
    l_g.start()
    l_w.start()

    barrier = pltpu.get_barrier_semaphore()

    def hello(dev):
        pl.semaphore_signal(barrier, inc=1, device_id=dev, device_id_type=MESH)

    hello(cdev)
    loop(T - 1, lambda i: hello(tdev(lax.rem(t + 1 + i, T))))
    loop(E - 1, lambda i: hello(edev(lax.rem(e + 1 + i, E))))

    b_rs = RingReduce(lambda k, h: bm.at[k, h], br, sent.at[0], ring_r.at[0], z, ring)
    b_ag = RingGather(bag, sent.at[1], ring_r.at[1], z, ring)
    p_rs = RingReduce(lambda k, h: pm.at[k, h], pr, sent.at[2], ring_r.at[2], z, ring)
    p_ag = RingGather(pag, sent.at[3], ring_r.at[3], z, ring)
    o_rs = RingReduce(lambda k, h: om.at[y * Z + k, h], orr, sent.at[4], ring_r.at[4], z, ring)

    def p_y(j):
        k = order(j)
        return rc(pt.at[k], py.at[k], sent.at[5], py_r.at[j], ydev)

    def o_y(j):
        k = order(j)
        return rc(om.at[(1 - y) * Z + k], oy.at[k], sent.at[6], oy_r.at[j], ydev)

    b_y = rc(bag.at[z, 0], bag.at[z, 1], sent.at[7], y_r.at[0], ydev)

    def p_add(j):
        p_y(j).wait_recv()
        k = order(j)
        pm[k] += py[k]

    def o_add(j):
        o_y(j).wait_recv()
        k = order(j)
        om[y * Z + k] += oy[k]

    def t_copy(n, ref, k):
        return rc(ref, ref, sent.at[9 + n], t_r.at[n], tdev(k))

    def t_send(n, ref):
        loop(T - 1, lambda i: t_copy(n, ref, lax.rem(t + 1 + i, T)).start())

    def t_all(n, some):
        return t_copy(n, some, lax.rem(t + 1, T))

    def z_copy(n, src, dst, k, side=0):
        return rc(src, dst, sent.at[11 + n], z_r.at[n], tdev((y + side - 2 * y * side) * Z + k))

    def z_others(body):
        loop(Z - 1, lambda i: body(lax.rem(z + 1 + i, Z)))

    def z_gather(n, arr):
        z_others(lambda k: z_copy(n, arr.at[z], arr.at[z], k).start())

    def z_all(n, some, side=0):
        return z_copy(n, some, some, lax.rem(z + 1, Z), side)

    def e_copy(n, src, dst, k):
        return rc(src, dst, sent.at[16 + n], e_r.at[n], edev(k))

    def e_others(body):
        loop(E - 1, lambda i: body(lax.rem(e + 1 + i, E)))

    def e_all(n, some):
        return e_copy(n, some, some, lax.rem(e + 1, E))

    def c_copy(n, src, dst):
        return rc(src, dst, sent.at[21 + n], c_r.at[n], cdev)

    l_u.wait()
    l_a.wait()
    ub[...] = uv[...].astype(BF16)
    blank = jnp.zeros((64, 128), BF16)

    def back(j):
        k = order(j)
        u1 = jnp.concatenate([ub[...], blank], axis=0)
        u2 = jnp.concatenate([blank, ub[...]], axis=0)
        v = dot_nt(av[0, k], u1) + dot_nt(av[1, k], u2)
        bm[k] = v.reshape(2, CH // 2, 128)

    loop(3, back)
    pl.semaphore_wait(barrier, T - 1 + E - 1 + 1)
    b_rs.begin(1)
    b_rs.begin(2)
    loop(Z, back, 3)

    l_d.wait()
    dd = dv[...]
    db[...] = jnp.where(y == 0, dd, swap(dd)).astype(BF16)

    def project(j):
        k = order(j)
        xload(j).wait()
        pa = dot(xv[0, k], db[...])
        pb = dot(xv[1, k], db[...])
        low = low_lanes(CH)
        pm[k] = jnp.where(low, pa, swap(pb)).reshape(2, CH // 2, 128)
        pt[k] = jnp.where(low, swap(pa), pb).reshape(2, CH // 2, 128)

    def project_send(j):
        project(j)
        p_y(j).start()

    loop(4, project_send)
    b_rs.step(1)
    loop(6, project_send, 4)
    loop(8, project, 6)
    p_add(0)
    p_rs.begin(1)

    l_h.wait()
    l_g.wait()
    hf = hv[...].astype(F32)
    sq = jnp.sum(hf * hf, axis=1, keepdims=True)
    sq = jnp.transpose(jnp.broadcast_to(sq, (256, 128)))
    rows[t, 0:1] = sq[0:1, 0:128]
    rows[t, 1:2] = sq[0:1, 128:256]
    t_send(0, rows.at[t])

    b_rs.step(2)
    p_add(1)
    b_rs.step(3)
    p_add(2)
    p_rs.begin(2)
    p_rs.step(1)
    b_rs.step(4)
    for h in range(2):
        bag[z, 0, h * 96 : (h + 1) * 96] = b_rs.result(h)
    b_ag.begin(0)
    b_y.start()
    loop(8, lambda j: p_y(j).start(), 6)

    def grad(p, k):
        cot = (bag[k, p] * delta_multiplier).astype(BF16)
        v = dot_tn(cot[:, :64], xv[0, k]) + dot_tn(cot[:, 64:], xv[1, k])
        gt[p, 0] += v[:, :512].reshape(8, 8, 512)
        gt[p, 1] += v[:, 512:].reshape(8, 8, 512)

    gt[...] = jnp.zeros_like(gt)
    both(0, lambda k: grad(0, k))

    t_all(0, rows.at[0:15]).wait_recv()
    mean = jnp.sum(rows[...], axis=0) / EMBED_DIMENSION
    scale = lax.rsqrt(mean + 1e-05)
    for i in range(2):
        half = slice(i * 128, (i + 1) * 128)
        col = jnp.transpose(jnp.broadcast_to(scale[i : i + 1], (128, 128)))
        for n in range(8):
            sl = slice(n * 128, (n + 1) * 128)
            normed[half, sl] = (hv[half, sl].astype(F32) * col * gv[:, sl]).astype(BF16)

    p_add(3)
    p_add(4)
    p_rs.step(2)
    b_ag.step(0, 1)
    b_y.wait_recv()
    b_ag.begin(1)

    def pack(v):
        return jnp.where(low_lanes(128), v[:128], v[128:]).reshape(8, 2, 8, 128)

    def twice(v, p):
        keep = low_lanes(256) if p == 0 else jnp.logical_not(low_lanes(256))
        v = jnp.where(keep, v, 0.0)
        return v + swap(v)

    def out_pair(i):
        v = dot(normed[...], wv[:, pl.ds(pl.multiple_of(i * 256, 256), 256)])
        om[2 * i, :, 0:128] = v[:, :128].reshape(2, 128, 128)
        om[2 * i + 1, :, 0:128] = v[:, 128:].reshape(2, 128, 128)

    dhi, dlo = split(dv[...])
    v = dot(normed[...], dhi) + dot(normed[...], dlo)
    for side in range(2):
        om[side * Z : side * Z + Z, :, 128:136] = pack(twice(v, side))
    l_w.wait()
    loop(4, lambda i: out_pair((1 - y) * 4 + i))
    loop(2, lambda j: o_y(j).start())
    both(1, lambda k: grad(0, k))
    b_ag.step(0, 2)
    p_add(5)
    p_add(6)
    p_rs.step(3)
    both(0, lambda k: grad(1, k))
    both(2, lambda k: grad(0, k))
    b_ag.step(1, 1)
    loop(3, lambda j: o_y(j).start(), 2)
    loop(4, lambda i: out_pair(y * 4 + i))
    b_ag.step(0, 3)
    p_add(7)
    p_rs.step(4)
    for h in range(2):
        pag[z, h] = p_rs.result(h)
    both(3, lambda k: grad(0, k))
    b_ag.step(1, 2)
    loop(4, lambda j: o_y(j).start(), 3)
    b_ag.step(0, 4)
    p_ag.begin(0)
    p_ag.begin(1)
    both(4, lambda k: grad(0, k))

    def g_core(p):
        return c_copy(p, gt.at[p, 1 - c], gc.at[p])

    def g_reduce(p):
        g_core(p).wait_recv()
        gt[p, c] += gc[p]
        gr[p, e] = gt[p, c, e]
        e_others(lambda k: e_copy(p, gt.at[p, c, k], gr.at[p, e], k).start())

    def g_gather(p):
        e_all(p, gr.at[p, 0:7]).wait_recv()
        gf[p, c, e] = jnp.sum(gr[p], axis=0)
        ref = gf.at[p, c, e]
        e_others(lambda k: e_copy(2 + p, ref, ref, k).start())

    def g_share(p):
        return c_copy(2 + p, gf.at[p, c], gf.at[p, c])

    def g_pass(p):
        e_all(2 + p, gf.at[p, c, 0:7]).wait_recv()
        g_share(p).start()

    def up_grad(k):
        pc = (pag[k].reshape(CH, 128) * delta_multiplier).astype(BF16)
        va = dot_tn(pc, av[0, k])
        vb = dot_tn(pc, av[1, k])
        gu[...] += (va[:64] + vb[64:]).reshape(8, 8, 128)

    def q_of(p):
        ghi, glo = split(jnp.concatenate([gf[p, 0].reshape(64, 512), gf[p, 1].reshape(64, 512)], axis=1))
        v = dot_nt(normed[...], jnp.concatenate([ghi, glo], axis=0))
        qg[p] = pack(v + swap(v)).reshape(8, 16, 128)

    theirs = [gf.at[p, 1 - c] for p in range(2)]

    g_core(0).start()
    both(1, lambda k: grad(1, k))
    gu[...] = jnp.zeros_like(gu)
    b_ag.step(1, 3)
    loop(6, lambda j: o_y(j).start(), 4)
    o_add(0)
    o_rs.begin(1)
    g_reduce(0)
    both(2, lambda k: grad(1, k))
    both(3, lambda k: grad(1, k))
    both(0, up_grad)
    b_ag.step(1, 4)
    both(4, lambda k: grad(1, k))
    g_core(1).start()
    p_ag.step(0, 1)
    p_ag.step(1, 1)
    o_add(1)
    o_add(2)
    o_rs.begin(2)
    both(1, up_grad)
    g_reduce(1)
    g_gather(0)
    o_rs.step(1)
    p_ag.step(0, 2)
    p_ag.step(1, 2)
    loop(7, lambda j: o_y(j).start(), 6)
    both(2, up_grad)
    o_add(3)
    o_add(4)
    o_rs.step(2)
    g_pass(0)
    g_gather(1)
    p_ag.step(0, 3)
    p_ag.step(1, 3)
    loop(8, lambda j: o_y(j).start(), 7)
    both(3, up_grad)
    c_copy(2, theirs[0], theirs[0]).wait_recv()
    q_of(0)
    qgr[0, z] = qg[0, z]
    z_others(lambda k: z_copy(3, qg.at[0, k], qgr.at[0, z], k).start())
    p_ag.step(0, 4)
    p_ag.step(1, 4)
    both(4, up_grad)
    gu_c = c_copy(4, gu, guc)
    gu_c.start()
    g_pass(1)
    o_add(5)
    o_add(6)
    gu_c.wait_recv()
    gur[e] = gu[...] + guc[...]
    e_others(lambda k: e_copy(4, gur.at[e], gur.at[e], k).start())
    c_copy(3, theirs[1], theirs[1]).wait_recv()
    q_of(1)
    loop(Z, lambda i: z_copy(4, qg.at[1, lax.rem(z + i, Z)], qgr.at[1, z], lax.rem(z + i, Z), 1).start())
    o_rs.step(3)
    g2 = jnp.sum(gf[...] * gf[...], axis=(0, 1, 2))
    tile = g2[:, 0:128] + g2[:, 128:256] + g2[:, 256:384] + g2[:, 384:512]
    o_add(7)
    e_all(4, gur.at[0:7]).wait_recv()
    guf[...] = jnp.sum(gur[...], axis=0)
    norms[t] = jnp.sum(tile + jnp.sum(guf[...] * guf[...], axis=0), axis=0, keepdims=True)
    t_send(1, norms.at[t])
    z_all(3, qgr.at[0, 0:7]).wait_recv()
    z_all(4, qgr.at[1], 1).wait_recv()
    qga[z] = jnp.sum(qgr[0], axis=0) + jnp.sum(qgr[1], axis=0)
    z_gather(2, qga)
    o_rs.step(4)
    for h in range(2):
        v = o_rs.result(h)
        base[h] = v[0:128]
        q0a[z, h * 8 : h * 8 + 8] = v[128:136]
    z_gather(1, q0a)
    t_all(1, norms.at[0:15]).wait_recv()
    total = jnp.sum(jnp.sum(norms[...], axis=0), keepdims=True)
    factor = jnp.minimum(1.0, clip_limit / (jnp.sqrt(total) + 1e-06))
    up = uv[...] - learning_rate * factor * guf[...].reshape(64, 128)
    zero = jnp.zeros_like(up)
    z_all(2, qga.at[0:7]).wait_recv()
    z_all(1, q0a.at[0:7]).wait_recv()
    q = q0a[...].reshape(128, 128) - learning_rate * factor * qga[...].reshape(128, 128)
    for h in range(2):
        wide = jnp.concatenate([up, zero] if h == 0 else [zero, up], axis=0)
        v = jnp.dot(q, wide, precision=lax.Precision.HIGHEST, preferred_element_type=F32)
        o_ref[:, h * 128 : (h + 1) * 128] = jnp.transpose(base[h] + delta_multiplier * v)

    for exchange in (b_rs, b_ag, p_rs, p_ag, o_rs):
        exchange.drain()
    rc(py, py, sent.at[5], py_r.at[0], ydev).wait_send()
    rc(oy, oy, sent.at[6], oy_r.at[0], ydev).wait_send()
    b_y.wait_send()
    t_all(0, rows.at[0:15]).wait_send()
    t_all(1, norms.at[0:15]).wait_send()
    z_all(1, q0a.at[0:7]).wait_send()
    z_all(2, qga.at[0:7]).wait_send()
    z_all(3, qgr.at[0, 0:7]).wait_send()
    z_all(4, qgr.at[1], 1).wait_send()
    for p in range(2):
        e_all(p, gr.at[p, 0:7]).wait_send()
        e_all(2 + p, gf.at[p, c, 0:7]).wait_send()
        g_core(p).wait_send()
        g_share(p).wait_send()
    e_all(4, gur.at[0:7]).wait_send()
    gu_c.wait_send()


def shards(x, a, w, d, u, hidden, gain):
    V = pltpu.VMEM
    dma = pltpu.SemaphoreType.DMA
    part = (8, 2, 96, 128)
    scratch = [
        V((2, 8, 192, 1024), BF16), V((2, 8, 192, 128), BF16), V((1024, 2048), BF16), V((1024, 128), F32),
        V((64, 128), F32), V((256, 1024), BF16), V((1, 1024), F32), V((1024, 128), BF16), V((64, 128), BF16),
        V(part, F32), V((14, 96, 128), F32), V((8, 2, 192, 128), F32),
        V(part, F32), V(part, F32), V(part, F32), V((14, 96, 128), F32), V(part, F32),
        V((16, 2, 136, 128), F32), V((8, 2, 136, 128), F32), V((14, 136, 128), F32),
        V((2, 2, 8, 8, 512), F32), V((2, 8, 8, 512), F32), V((2, 8, 8, 512), F32), V((2, 2, 8, 8, 512), F32),
        V((8, 8, 128), F32), V((8, 8, 128), F32), V((8, 8, 8, 128), F32), V((8, 8, 128), F32),
        V((16, 2, 128), F32), V((16, 1, 128), F32), V((256, 1024), BF16), V((2, 128, 128), F32),
        V((8, 16, 128), F32),
        V((2, 8, 16, 128), F32), V((2, 8, 16, 128), F32), V((8, 16, 128), F32),
        dma((6,)), dma((8,)), dma((5, 14)), dma((8,)), dma((8,)), dma((2,)),
        dma((2,)), dma((5,)), dma((5,)), dma((5,)), dma((26,)),
    ]
    return pl.pallas_call(
        kernel,
        out_shape=jax.ShapeDtypeStruct((128, 256), F32),
        in_specs=[pl.BlockSpec(memory_space=pl.ANY)] * 7,
        out_specs=pl.BlockSpec(memory_space=pltpu.VMEM),
        scratch_shapes=scratch,
        compiler_params=pltpu.CompilerParams(
            collective_id=0, has_side_effects=True, vmem_limit_bytes=56 << 20
        ),
    )(x.reshape(2, 8, CH, 1024), a.reshape(2, 8, CH, 128), w, d, u, hidden, gain.reshape(1, 1024))


def solution(mesh):
    placed = (
        P("dp", "tensor"),
        P("dp", "tensor"),
        P("tensor", None),
        P("tensor", None),
        P(None, "tensor"),
        P("dp", "tensor"),
        P("tensor"),
    )
    return jax.shard_map(
        shards, mesh=mesh, in_specs=placed, out_specs=P("tensor", "dp"), check_vma=False
    )
```

```python
import functools

import jax
import jax.numpy as jnp
from jax import lax
from jax.experimental import pallas as pl
from jax.experimental.pallas import tpu as pltpu
from jax.sharding import PartitionSpec as P

MESH = pl.DeviceIdType.MESH
F32 = jnp.float32
BF16 = jnp.bfloat16

EMBED_DIMENSION = 16384
delta_multiplier = 2.0
learning_rate = 4.0
clip_limit = 1.0

Z = 8
T = 16
E = 8
CH = 192


def rc(src, dst, ss, rs, dev):
    return pltpu.make_async_remote_copy(
        src_ref=src, dst_ref=dst, send_sem=ss, recv_sem=rs, device_id=dev, device_id_type=MESH
    )


def low_lanes(rows):
    return lax.broadcasted_iota(jnp.int32, (rows, 128), 1) < 64


def swap(v):
    return pltpu.roll(v, 64, 1)


def dot(a, b):
    return jnp.dot(a, b, preferred_element_type=F32)


def dot_nt(a, b):
    return lax.dot_general(a, b, (((1,), (1,)), ((), ())), preferred_element_type=F32)


def dot_tn(a, b):
    return lax.dot_general(a, b, (((0,), (0,)), ((), ())), preferred_element_type=F32)


def split(v):
    hi = v.astype(BF16)
    return hi, (v - hi.astype(F32)).astype(BF16)


class RingReduce:
    def __init__(self, own, buf, ss, rs, z, dev):
        self.own, self.buf, self.ss, self.rs, self.z, self.dev = own, buf, ss, rs, z, dev

    def chunk(self, d, far):
        return lax.rem(self.z + (far if d == 0 else Z - far), Z)

    def slot(self, d, h, s):
        return d * 7 + (s - 1 if d == h else 4 + s - 2)

    def copy(self, d, h, s):
        first = 1 if d == h else 2
        if s == first:
            src = self.own(self.chunk(d, 5 - s), h)
        else:
            src = self.buf.at[self.slot(d, h, s - 1)]
        i = self.slot(d, h, s)
        return rc(src, self.buf.at[i], self.ss, self.rs.at[i], self.dev(d))

    def begin(self, first):
        for d in range(2):
            h = d if first == 1 else 1 - d
            self.copy(d, h, first).start()

    def step(self, s):
        for same in (True, False):
            if s == 1 and not same:
                continue
            for d in range(2):
                h = d if same else 1 - d
                self.copy(d, h, s).wait_recv()
                if s < 4:
                    self.buf[self.slot(d, h, s)] += self.own(self.chunk(d, 4 - s), h)[...]
                    self.copy(d, h, s + 1).start()

    def result(self, h):
        return self.own(self.z, h)[...] + (self.buf[self.slot(0, h, 4)] + self.buf[self.slot(1, h, 4)])

    def drain(self):
        rc(self.buf, self.buf, self.ss, self.rs.at[0], self.dev(0)).wait_send()


class RingGather:
    def __init__(self, arr, ss, rs, z, dev, dev2):
        self.arr, self.ss, self.rs, self.z, self.dev, self.dev2 = arr, ss, rs, z, dev, dev2

    def copy(self, d, p, s):
        k = lax.rem(self.z + (0, Z - 1, Z - 2, Z - 2)[s - 1] if d == 0 else self.z + (0, 1, 2, 2)[s - 1], Z)
        ref = self.arr.at[k, p]
        i = d * 7 + (s - 1 if d == p else 4 + s - 1)
        return rc(ref, ref, self.ss, self.rs.at[i], (self.dev2 if s == 4 else self.dev)(d))

    def begin(self):
        for p in range(2):
            for d in range(2):
                self.copy(d, p, 1).start()

    def step(self, s):
        for same in (True, False):
            for d in range(2):
                p = d if same else 1 - d
                self.copy(d, p, s).wait_recv()
                if s == 2 and same:
                    self.copy(d, p, 4).start()
                if s < 3:
                    self.copy(d, p, s + 1).start()
        if s == 3:
            for d in range(2):
                self.copy(d, d, 4).wait_recv()

    def drain(self):
        all_sent = self.arr.at[0:7]
        rc(all_sent, all_sent, self.ss, self.rs.at[0], self.dev(0)).wait_send()


class ShortRingReduce:
    def __init__(self, own, buf, ss, rs, z, dev, dev2):
        self.own, self.buf, self.ss, self.rs, self.z, self.dev, self.dev2 = own, buf, ss, rs, z, dev, dev2

    def chunk(self, d, far):
        return lax.rem(self.z + (far if d == 0 else Z - far), Z)

    def copy(self, d, h, s):
        i = d * 7 + 2 * s - 1 + h
        src = self.own(self.chunk(d, 3), h) if s == 1 else self.buf.at[i - 2]
        return rc(src, self.buf.at[i], self.ss, self.rs.at[i], self.dev(d))

    def antipode(self, d):
        i = d * 7
        return rc(self.own(self.chunk(d, 4), d), self.buf.at[i], self.ss, self.rs.at[i], self.dev2(d))

    def begin(self, same):
        for d in range(2):
            self.copy(d, d if same else 1 - d, 1).start()

    def step(self, s):
        for same in (True, False):
            for d in range(2):
                h = d if same else 1 - d
                self.copy(d, h, s).wait_recv()
                if s == 3:
                    continue
                v = self.own(self.chunk(d, 3 - s), h)[...]
                if s == 1 and same:
                    self.antipode(d).wait_recv()
                    v = v + self.buf[d * 7]
                self.buf[d * 7 + 2 * s - 1 + h] += v
                self.copy(d, h, s + 1).start()

    def result(self, h):
        return self.own(self.z, h)[...] + (self.buf[5 + h] + self.buf[12 + h])

    def drain(self):
        rc(self.buf, self.buf, self.ss, self.rs.at[0], self.dev(0)).wait_send()


class PairRingGather:
    def __init__(self, arr, ss, ss4, rs, z, dev):
        self.arr, self.ss, self.ss4, self.rs, self.z, self.dev = arr, ss, ss4, rs, z, dev

    def copy(self, d, p, s):
        k = lax.rem(self.z + (Z - s + 1 if d == 0 else s - 1), Z)
        ref = self.arr.at[k, p, d * 96 : d * 96 + 96] if s == 4 else self.arr.at[k, p]
        return rc(ref, ref, self.ss4 if s == 4 else self.ss, self.rs.at[d * 6 + p * 4 + s - 1], self.dev(d))

    def begin(self, p):
        for d in range(2):
            self.copy(d, p, 1).start()

    def step(self, p, s):
        for d in range(2):
            self.copy(d, p, s).wait_recv()
            if s < (4, 2)[p]:
                self.copy(d, p, s + 1).start()

    def drain(self):
        for ref, ss in ((self.arr.at[0:5], self.ss), (self.arr.at[0, 0], self.ss4)):
            rc(ref, ref, ss, self.rs.at[0], self.dev(0)).wait_send()


def kernel(
    x_hbm, a_hbm, w_hbm, d_hbm, u_hbm, h_hbm, gain_hbm, o_ref,
    xv, av, wv, dv, uv, hv, gv, db, ub,
    bm, br, bag, pm, pt, py, pr, pag, om, oy, orr,
    gt, gr, gh, gf, gu, gur, guh, guf, rows, norms, normed, base,
    q0, q0y, q0r, q0a, qg, qgr, qga,
    ld, ls, xs, ring_r, py_r, oy_r, y_r, t_r, z_r, w_r, h_r, sent,
):
    dpi = lax.axis_index("dp")
    t = lax.axis_index("tensor")
    e, c = dpi // 2, lax.rem(dpi, 2)
    xx, yh = e // 2, lax.rem(e, 2)
    y, z = t // Z, lax.rem(t, Z)
    zdev = (dpi, y * Z + lax.rem(z + 1, Z)), (dpi, y * Z + lax.rem(z + Z - 1, Z))
    ydev = (dpi, (1 - y) * Z + z)
    w = xx * 2 + c
    hdev = ((xx * 2 + 1 - yh) * 2 + c, t)

    def ring(d):
        return zdev[d]

    def ring2(d):
        return (dpi, y * Z + lax.rem(z + (2 if d == 0 else Z - 2), Z))

    def tdev(k):
        return (dpi, k)

    def wdev(k):
        return ((k // 2 * 2 + yh) * 2 + lax.rem(k, 2), t)

    def order(j):
        far = 4 - (j + 1) // 2
        return lax.rem(z + (1 - 2 * lax.rem(j + 1, 2)) * far + Z, Z)

    def loop(n, body, first=0):
        def step(i, carry):
            body(i)
            return carry

        lax.fori_loop(first, n, step, 0)

    def both(far, body):
        if far in (0, 4):
            body(lax.rem(z + far, Z))
        else:
            loop(2, lambda i: body(lax.rem(z + far + i * (Z - 2 * far), Z)))

    def local(src, dst, i):
        return pltpu.make_async_copy(src, dst, ld.at[i])

    l_u, l_d = local(u_hbm, uv, 0), local(d_hbm, dv, 1)
    l_h, l_g, l_w = local(h_hbm, hv, 2), local(gain_hbm, gv, 3), local(w_hbm, wv, 4)

    def aload(j):
        k = order(j)
        return pltpu.make_async_copy(a_hbm.at[:, k], av.at[:, k], ls.at[j])


    def xload(j):
        k = order(j)
        return pltpu.make_async_copy(x_hbm.at[:, k], xv.at[:, k], xs.at[j])

    barrier = pltpu.get_barrier_semaphore()

    def hello(dev):
        pl.semaphore_signal(barrier, inc=1, device_id=dev, device_id_type=MESH)

    hello(hdev)
    loop(T - 1, lambda i: hello(tdev(lax.rem(t + 1 + i, T))))
    l_u.start()
    loop(Z, lambda j: aload(j).start())
    l_d.start()
    loop(E - 1, lambda i: hello(wdev(lax.rem(w + 1 + i, E))))
    loop(Z, lambda j: xload(j).start())
    l_h.start()
    l_g.start()
    l_w.start()

    b_rs = ShortRingReduce(lambda k, h: bm.at[k, h], br, sent.at[0], ring_r.at[0], z, ring, ring2)
    b_ag = PairRingGather(bag, sent.at[1], sent.at[27], ring_r.at[1], z, ring)
    p_rs = ShortRingReduce(lambda k, h: pm.at[k, h], pr, sent.at[2], ring_r.at[2], z, ring, ring2)
    p_ag = RingGather(pag, sent.at[3], ring_r.at[3], z, ring, ring2)
    o_rs = RingReduce(lambda k, h: om.at[y * Z + k, h], orr, sent.at[4], ring_r.at[4], z, ring)

    def p_y(j):
        k = order(j)
        return rc(pt.at[k], py.at[k], sent.at[5], py_r.at[j], ydev)

    def o_y(j):
        k = order(j)
        return rc(om.at[(1 - y) * Z + k], oy.at[k], sent.at[6], oy_r.at[j], ydev)

    b_y = rc(bag.at[z, 0], bag.at[z, 1], sent.at[7], y_r.at[0], ydev)

    def b_far(far):
        k = lax.rem(z + far, Z)
        return rc(bag.at[k, 0], bag.at[k, 1], sent.at[25 + far], y_r.at[far - 1], ydev)

    q0_y = rc(q0.at[1], q0y, sent.at[8], y_r.at[1], ydev)

    def p_add(j):
        p_y(j).wait_recv()
        k = order(j)
        pm[k] += py[k]

    def o_add(j):
        o_y(j).wait_recv()
        k = order(j)
        om[y * Z + k] += oy[k]

    def t_copy(n, ref, k):
        return rc(ref, ref, sent.at[9 + n], t_r.at[n], tdev(k))

    def t_send(n, ref):
        loop(T - 1, lambda i: t_copy(n, ref, lax.rem(t + 1 + i, T)).start())

    def t_all(n, some):
        return t_copy(n, some, lax.rem(t + 1, T))

    def z_copy(n, src, dst, k, side=0):
        return rc(src, dst, sent.at[11 + n], z_r.at[n], tdev((y + side - 2 * y * side) * Z + k))

    def z_others(body):
        loop(Z - 1, lambda i: body(lax.rem(z + 1 + i, Z)))

    def z_gather(n, arr):
        z_others(lambda k: z_copy(n, arr.at[z], arr.at[z], k).start())

    def z_all(n, some, side=0):
        return z_copy(n, some, some, lax.rem(z + 1, Z), side)

    def w_copy(n, src, dst, k):
        return rc(src, dst, sent.at[16 + n], w_r.at[n], wdev(k))

    def w_others(body):
        loop(E - 1, lambda i: body(lax.rem(w + 1 + i, E)))

    def w_all(n, some):
        return w_copy(n, some, some, lax.rem(w + 1, E))

    def h_copy(n, src, dst):
        return rc(src, dst, sent.at[21 + n], h_r.at[n], hdev)

    l_u.wait()
    ub[...] = uv[...].astype(BF16)
    blank = jnp.zeros((64, 128), BF16)

    def back(j):
        aload(j).wait()
        k = order(j)
        u1 = jnp.concatenate([ub[...], blank], axis=0)
        u2 = jnp.concatenate([blank, ub[...]], axis=0)
        v = dot_nt(av[0, k], u1) + dot_nt(av[1, k], u2)
        bm[k] = v.reshape(2, CH // 2, 128)

    back(0)
    pl.semaphore_wait(barrier, T - 1 + E - 1 + 1)
    for d in range(2):
        b_rs.antipode(d).start()
    loop(3, back, 1)
    b_rs.begin(True)
    b_rs.begin(False)

    l_d.wait()
    dd = dv[...]
    db[...] = jnp.where(y == 0, dd, swap(dd)).astype(BF16)

    def project(j):
        k = order(j)
        xload(j).wait()
        pa = dot(xv[0, k], db[...])
        pb = dot(xv[1, k], db[...])
        low = low_lanes(CH)
        pm[k] = jnp.where(low, pa, swap(pb)).reshape(2, CH // 2, 128)
        pt[k] = jnp.where(low, swap(pa), pb).reshape(2, CH // 2, 128)

    def project_send(j):
        project(j)
        p_y(j).start()

    loop(4, project_send)
    loop(Z, back, 3)

    l_h.wait()
    l_g.wait()
    hf = hv[...].astype(F32)
    sq = jnp.sum(hf * hf, axis=1, keepdims=True)
    sq = jnp.transpose(jnp.broadcast_to(sq, (256, 128)))
    rows[t, 0:1] = sq[0:1, 0:128]
    rows[t, 1:2] = sq[0:1, 128:256]
    t_send(0, rows.at[t])

    loop(5, project_send, 4)
    b_rs.step(1)
    loop(6, project_send, 5)
    loop(8, project, 6)
    b_rs.step(2)
    p_add(0)
    p_add(1)
    p_add(2)
    for d in range(2):
        p_rs.antipode(d).start()
    p_rs.begin(True)
    b_rs.step(3)
    for h in range(2):
        bag[z, 0, h * 96 : (h + 1) * 96] = b_rs.result(h)
    b_ag.begin(0)
    b_y.start()
    loop(8, lambda j: p_y(j).start(), 6)
    p_rs.begin(False)

    def grad(p, k):
        cot = (bag[k, p] * delta_multiplier).astype(BF16)
        v = dot_tn(cot[:, :64], xv[0, k]) + dot_tn(cot[:, 64:], xv[1, k])
        gt[p] += v.reshape(8, 8, 1024)

    gt[...] = jnp.zeros_like(gt)
    both(0, lambda k: grad(0, k))

    t_all(0, rows.at[0:15]).wait_recv()
    mean = jnp.sum(rows[...], axis=0) / EMBED_DIMENSION
    scale = lax.rsqrt(mean + 1e-05)
    for i in range(2):
        half = slice(i * 128, (i + 1) * 128)
        col = jnp.transpose(jnp.broadcast_to(scale[i : i + 1], (128, 128)))
        for n in range(8):
            sl = slice(n * 128, (n + 1) * 128)
            normed[half, sl] = (hv[half, sl].astype(F32) * col * gv[:, sl]).astype(BF16)

    def pack(v):
        return jnp.where(low_lanes(128), v[:128], v[128:]).reshape(8, 16, 128)

    def twice(v, p):
        keep = low_lanes(256) if p == 0 else jnp.logical_not(low_lanes(256))
        v = jnp.where(keep, v, 0.0)
        return v + swap(v)

    def out_pair(i):
        v = dot(normed[...], wv[:, pl.ds(pl.multiple_of(i * 256, 256), 256)])
        om[2 * i] = v[:, :128].reshape(2, 128, 128)
        om[2 * i + 1] = v[:, 128:].reshape(2, 128, 128)

    dhi, dlo = split(jnp.where(y == 0, dv[...], swap(dv[...])))
    v = dot(normed[...], dhi) + dot(normed[...], dlo)
    for side in range(2):
        q0[side] = pack(twice(v, side))
    q0_y.start()
    l_w.wait()
    loop(4, lambda i: out_pair((1 - y) * 4 + i))
    loop(2, lambda j: o_y(j).start())
    b_ag.step(0, 1)
    b_y.wait_recv()
    b_ag.begin(1)
    both(1, lambda k: grad(0, k))
    both(0, lambda k: grad(1, k))
    p_add(3)
    p_add(4)
    b_ag.step(0, 2)
    p_rs.step(1)
    both(2, lambda k: grad(0, k))
    b_ag.step(1, 1)
    loop(4, lambda i: out_pair(y * 4 + i))
    p_add(5)
    p_add(6)
    b_ag.step(0, 3)
    b_far(3).start()
    b_far(5).start()
    p_rs.step(2)
    both(3, lambda k: grad(0, k))
    both(1, lambda k: grad(1, k))
    b_ag.step(0, 4)
    b_far(4).start()
    loop(4, lambda j: o_y(j).start(), 2)
    both(4, lambda k: grad(0, k))

    def g_reduce(p):
        gr[p, w] = gt[p, w]
        w_others(lambda k: w_copy(p, gt.at[p, k], gr.at[p, w], k).start())

    def g_cross(p):
        w_all(p, gr.at[p, 0:7]).wait_recv()
        gh[p, 0] = jnp.sum(gr[p], axis=0)
        h_copy(p, gh.at[p, 0], gh.at[p, 1]).start()

    def g_gather(p):
        h_copy(p, gh.at[p, 0], gh.at[p, 1]).wait_recv()
        gf[p, w] = gh[p, 0] + gh[p, 1]
        w_others(lambda k: w_copy(2 + p, gf.at[p, w], gf.at[p, w], k).start())

    def g_all(p):
        return w_all(2 + p, gf.at[p, 0:7])

    def up_grad(k):
        pc = (pag[k].reshape(CH, 128) * delta_multiplier).astype(BF16)
        va = dot_tn(pc, av[0, k])
        vb = dot_tn(pc, av[1, k])
        gu[...] += (va[:64] + vb[64:]).reshape(8, 8, 128)

    def q_of(p):
        ghi, glo = split(gf[p].reshape(64, 1024))
        v = dot_nt(normed[...], jnp.concatenate([ghi, glo], axis=0))
        qg[p] = pack(v + swap(v))

    g_reduce(0)
    gu[...] = jnp.zeros_like(gu)
    p_add(7)
    p_rs.step(3)
    for h in range(2):
        pag[z, h] = p_rs.result(h)
    p_ag.begin()
    o_add(0)
    o_rs.begin(1)
    b_ag.step(1, 2)
    both(2, lambda k: grad(1, k))
    b_far(3).wait_recv()
    b_far(5).wait_recv()
    both(3, lambda k: grad(1, k))
    b_far(4).wait_recv()
    both(4, lambda k: grad(1, k))
    g_reduce(1)
    p_ag.step(1)
    g_cross(0)
    loop(5, lambda j: o_y(j).start(), 4)
    both(0, up_grad)
    both(1, up_grad)
    o_add(1)
    o_add(2)
    o_rs.begin(2)
    p_ag.step(2)
    g_cross(1)
    loop(6, lambda j: o_y(j).start(), 5)
    both(2, up_grad)
    g_gather(0)
    g_gather(1)
    loop(7, lambda j: o_y(j).start(), 6)
    o_rs.step(1)
    p_ag.step(3)
    both(3, up_grad)
    both(4, up_grad)
    gur[w] = gu[...]
    w_others(lambda k: w_copy(4, gur.at[w], gur.at[w], k).start())
    loop(8, lambda j: o_y(j).start(), 7)
    q0_y.wait_recv()
    q0[0] += q0y[...]
    q0r[z] = q0[0, z]
    z_others(lambda k: z_copy(0, q0.at[0, k], q0r.at[z], k).start())
    g_all(0).wait_recv()
    q_of(0)
    qgr[0, z] = qg[0, z]
    z_others(lambda k: z_copy(3, qg.at[0, k], qgr.at[0, z], k).start())
    o_add(3)
    o_add(4)
    o_rs.step(2)
    g_all(1).wait_recv()
    q_of(1)
    loop(Z, lambda i: z_copy(4, qg.at[1, lax.rem(z + i, Z)], qgr.at[1, z], lax.rem(z + i, Z), 1).start())
    w_all(4, gur.at[0:7]).wait_recv()
    guh[0] = jnp.sum(gur[...], axis=0)
    gu_h = h_copy(2, guh.at[0], guh.at[1])
    gu_h.start()
    g2 = jnp.sum(gf[...] * gf[...], axis=(0, 1))
    tile = g2[:, 0:128]
    for i in range(1, 8):
        tile = tile + g2[:, i * 128 : (i + 1) * 128]
    z_all(0, q0r.at[0:7]).wait_recv()
    q0a[z] = jnp.sum(q0r[...], axis=0)
    z_gather(1, q0a)
    o_add(5)
    o_add(6)
    o_rs.step(3)
    gu_h.wait_recv()
    guf[...] = guh[0] + guh[1]
    norms[t] = jnp.sum(tile + jnp.sum(guf[...] * guf[...], axis=0), axis=0, keepdims=True)
    t_send(1, norms.at[t])
    z_all(3, qgr.at[0, 0:7]).wait_recv()
    z_all(4, qgr.at[1], 1).wait_recv()
    qga[z] = jnp.sum(qgr[0], axis=0) + jnp.sum(qgr[1], axis=0)
    z_gather(2, qga)
    o_add(7)
    o_rs.step(4)
    for h in range(2):
        base[h] = o_rs.result(h)
    t_all(1, norms.at[0:15]).wait_recv()
    total = jnp.sum(jnp.sum(norms[...], axis=0), keepdims=True)
    factor = jnp.minimum(1.0, clip_limit / (jnp.sqrt(total) + 1e-06))
    up = uv[...] - learning_rate * factor * guf[...].reshape(64, 128)
    zero = jnp.zeros_like(up)
    z_all(1, q0a.at[0:7]).wait_recv()
    z_all(2, qga.at[0:7]).wait_recv()
    q = q0a[...].reshape(128, 128) - learning_rate * factor * qga[...].reshape(128, 128)
    for h in range(2):
        wide = jnp.concatenate([up, zero] if h == 0 else [zero, up], axis=0)
        v = jnp.dot(q, wide, precision=lax.Precision.HIGHEST, preferred_element_type=F32)
        o_ref[:, h * 128 : (h + 1) * 128] = jnp.transpose(base[h] + delta_multiplier * v)

    for exchange in (b_rs, b_ag, p_rs, p_ag, o_rs):
        exchange.drain()
    rc(py, py, sent.at[5], py_r.at[0], ydev).wait_send()
    rc(oy, oy, sent.at[6], oy_r.at[0], ydev).wait_send()
    b_y.wait_send()
    for far in (3, 4, 5):
        b_far(far).wait_send()
    q0_y.wait_send()
    z_all(0, q0r.at[0:7]).wait_send()
    t_all(0, rows.at[0:15]).wait_send()
    t_all(1, norms.at[0:15]).wait_send()
    z_all(1, q0a.at[0:7]).wait_send()
    z_all(2, qga.at[0:7]).wait_send()
    z_all(3, qgr.at[0, 0:7]).wait_send()
    z_all(4, qgr.at[1], 1).wait_send()
    for p in range(2):
        w_all(p, gr.at[p, 0:7]).wait_send()
        g_all(p).wait_send()
        h_copy(p, gh.at[p, 0], gh.at[p, 1]).wait_send()
    w_all(4, gur.at[0:7]).wait_send()
    gu_h.wait_send()


def shards(x, a, w, d, u, hidden, gain):
    V = pltpu.VMEM
    dma = pltpu.SemaphoreType.DMA
    part = (8, 2, 96, 128)
    scratch = [
        V((2, 8, 192, 1024), BF16), V((2, 8, 192, 128), BF16), V((1024, 2048), BF16), V((1024, 128), F32),
        V((64, 128), F32), V((256, 1024), BF16), V((1, 1024), F32), V((1024, 128), BF16), V((64, 128), BF16),
        V(part, F32), V((14, 96, 128), F32), V((8, 2, 192, 128), F32),
        V(part, F32), V(part, F32), V(part, F32), V((14, 96, 128), F32), V(part, F32),
        V((16, 2, 128, 128), F32), V((8, 2, 128, 128), F32), V((14, 128, 128), F32),
        V((2, 8, 8, 1024), F32), V((2, 8, 8, 1024), F32), V((2, 2, 8, 1024), F32), V((2, 8, 8, 1024), F32),
        V((8, 8, 128), F32), V((8, 8, 8, 128), F32), V((2, 8, 8, 128), F32), V((8, 8, 128), F32),
        V((16, 2, 128), F32), V((16, 1, 128), F32), V((256, 1024), BF16), V((2, 128, 128), F32),
        V((2, 8, 16, 128), F32), V((8, 16, 128), F32), V((8, 16, 128), F32), V((8, 16, 128), F32),
        V((2, 8, 16, 128), F32), V((2, 8, 16, 128), F32), V((8, 16, 128), F32),
        dma((5,)), dma((8,)), dma((8,)), dma((5, 14)), dma((8,)), dma((8,)), dma((5,)),
        dma((2,)), dma((5,)), dma((5,)), dma((3,)), dma((31,)),
    ]
    return pl.pallas_call(
        kernel,
        out_shape=jax.ShapeDtypeStruct((128, 256), F32),
        in_specs=[pl.BlockSpec(memory_space=pl.ANY)] * 7,
        out_specs=pl.BlockSpec(memory_space=pltpu.VMEM),
        scratch_shapes=scratch,
        compiler_params=pltpu.CompilerParams(
            collective_id=0, has_side_effects=True, vmem_limit_bytes=56 << 20
        ),
    )(x.reshape(2, 8, CH, 1024), a.reshape(2, 8, CH, 128), w, d, u, hidden, gain.reshape(1, 1024))


def solution(mesh):
    placed = (
        P("dp", "tensor"),
        P("dp", "tensor"),
        P("tensor", None),
        P("tensor", None),
        P(None, "tensor"),
        P("dp", "tensor"),
        P("tensor"),
    )
    return jax.shard_map(
        shards, mesh=mesh, in_specs=placed, out_specs=P("tensor", "dp"), check_vma=False
    )
```

```python
import functools

import jax
import jax.numpy as jnp
from jax import lax
from jax.experimental import pallas as pl
from jax.experimental.pallas import tpu as pltpu
from jax.sharding import PartitionSpec as P

MESH = pl.DeviceIdType.MESH
F32 = jnp.float32
BF16 = jnp.bfloat16

EMBED_DIMENSION = 16384
delta_multiplier = 2.0
learning_rate = 4.0
clip_limit = 1.0

Z = 8
T = 16
E = 8
CH = 192


def rc(src, dst, ss, rs, dev):
    return pltpu.make_async_remote_copy(
        src_ref=src, dst_ref=dst, send_sem=ss, recv_sem=rs, device_id=dev, device_id_type=MESH
    )


def low_lanes(rows):
    return lax.broadcasted_iota(jnp.int32, (rows, 128), 1) < 64


def swap(v):
    return pltpu.roll(v, 64, 1)


def dot(a, b):
    return jnp.dot(a, b, preferred_element_type=F32)


def dot_nt(a, b):
    return lax.dot_general(a, b, (((1,), (1,)), ((), ())), preferred_element_type=F32)


def dot_tn(a, b):
    return lax.dot_general(a, b, (((0,), (0,)), ((), ())), preferred_element_type=F32)


def split(v):
    hi = v.astype(BF16)
    return hi, (v - hi.astype(F32)).astype(BF16)


class RingReduce:
    def __init__(self, own, buf, ss, rs, z, dev):
        self.own, self.buf, self.ss, self.rs, self.z, self.dev = own, buf, ss, rs, z, dev

    def chunk(self, d, far):
        return lax.rem(self.z + (far if d == 0 else Z - far), Z)

    def slot(self, d, h, s):
        return d * 7 + (s - 1 if d == h else 4 + s - 2)

    def copy(self, d, h, s):
        first = 1 if d == h else 2
        if s == first:
            src = self.own(self.chunk(d, 5 - s), h)
        else:
            src = self.buf.at[self.slot(d, h, s - 1)]
        i = self.slot(d, h, s)
        return rc(src, self.buf.at[i], self.ss, self.rs.at[i], self.dev(d))

    def begin(self, first):
        for d in range(2):
            h = d if first == 1 else 1 - d
            self.copy(d, h, first).start()

    def step(self, s):
        for same in (True, False):
            if s == 1 and not same:
                continue
            for d in range(2):
                h = d if same else 1 - d
                self.copy(d, h, s).wait_recv()
                if s < 4:
                    self.buf[self.slot(d, h, s)] += self.own(self.chunk(d, 4 - s), h)[...]
                    self.copy(d, h, s + 1).start()

    def result(self, h):
        return self.own(self.z, h)[...] + (self.buf[self.slot(0, h, 4)] + self.buf[self.slot(1, h, 4)])

    def drain(self):
        rc(self.buf, self.buf, self.ss, self.rs.at[0], self.dev(0)).wait_send()


class RingGather:
    def __init__(self, arr, ss, rs, z, dev, dev2):
        self.arr, self.ss, self.rs, self.z, self.dev, self.dev2 = arr, ss, rs, z, dev, dev2

    def copy(self, d, p, s):
        k = lax.rem(self.z + (0, Z - 1, Z - 2, Z - 2)[s - 1] if d == 0 else self.z + (0, 1, 2, 2)[s - 1], Z)
        ref = self.arr.at[k, p]
        i = d * 7 + (s - 1 if d == p else 4 + s - 1)
        return rc(ref, ref, self.ss, self.rs.at[i], (self.dev2 if s == 4 else self.dev)(d))

    def begin(self):
        for p in range(2):
            for d in range(2):
                self.copy(d, p, 1).start()

    def step(self, s):
        for same in (True, False):
            for d in range(2):
                p = d if same else 1 - d
                self.copy(d, p, s).wait_recv()
                if s == 2 and same:
                    self.copy(d, p, 4).start()
                if s < 3:
                    self.copy(d, p, s + 1).start()
        if s == 3:
            for d in range(2):
                self.copy(d, d, 4).wait_recv()

    def drain(self):
        all_sent = self.arr.at[0:7]
        rc(all_sent, all_sent, self.ss, self.rs.at[0], self.dev(0)).wait_send()


class ShortRingReduce:
    def __init__(self, own, buf, ss, rs, z, dev, dev2):
        self.own, self.buf, self.ss, self.rs, self.z, self.dev, self.dev2 = own, buf, ss, rs, z, dev, dev2

    def chunk(self, d, far):
        return lax.rem(self.z + (far if d == 0 else Z - far), Z)

    def copy(self, d, h, s):
        i = d * 7 + 2 * s - 1 + h
        src = self.own(self.chunk(d, 3), h) if s == 1 else self.buf.at[i - 2]
        return rc(src, self.buf.at[i], self.ss, self.rs.at[i], self.dev(d))

    def antipode(self, d):
        i = d * 7
        return rc(self.own(self.chunk(d, 4), d), self.buf.at[i], self.ss, self.rs.at[i], self.dev2(d))

    def begin(self, same):
        for d in range(2):
            self.copy(d, d if same else 1 - d, 1).start()

    def step(self, s):
        for same in (True, False):
            for d in range(2):
                h = d if same else 1 - d
                self.copy(d, h, s).wait_recv()
                if s == 3:
                    continue
                v = self.own(self.chunk(d, 3 - s), h)[...]
                if s == 1 and same:
                    self.antipode(d).wait_recv()
                    v = v + self.buf[d * 7]
                self.buf[d * 7 + 2 * s - 1 + h] += v
                self.copy(d, h, s + 1).start()

    def result(self, h):
        return self.own(self.z, h)[...] + (self.buf[5 + h] + self.buf[12 + h])

    def drain(self):
        rc(self.buf, self.buf, self.ss, self.rs.at[0], self.dev(0)).wait_send()


class PairRingGather:
    def __init__(self, arr, ss, ss4, rs, z, dev):
        self.arr, self.ss, self.ss4, self.rs, self.z, self.dev = arr, ss, ss4, rs, z, dev

    def copy(self, d, p, s):
        k = lax.rem(self.z + (Z - s + 1 if d == 0 else s - 1), Z)
        ref = self.arr.at[k, p, d * 96 : d * 96 + 96] if s == 4 else self.arr.at[k, p]
        return rc(ref, ref, self.ss4 if s == 4 else self.ss, self.rs.at[d * 6 + p * 4 + s - 1], self.dev(d))

    def begin(self, p):
        for d in range(2):
            self.copy(d, p, 1).start()

    def step(self, p, s):
        for d in range(2):
            self.copy(d, p, s).wait_recv()
            if s < (4, 2)[p]:
                self.copy(d, p, s + 1).start()

    def drain(self):
        for ref, ss in ((self.arr.at[0:5], self.ss), (self.arr.at[0, 0], self.ss4)):
            rc(ref, ref, ss, self.rs.at[0], self.dev(0)).wait_send()


def kernel(
    x_hbm, a_hbm, w_hbm, d_hbm, u_hbm, h_hbm, gain_hbm, o_ref,
    xv, av, wv, dv, uv, hv, gv, db, ub,
    bm, br, bag, pm, pt, py, pr, pag, om, oy, orr,
    gt, gr, gh, gf, gu, gur, guh, guf, rows, norms, normed, base,
    q0, q0y, q0r, q0a, qg, qgr, qga,
    ld, ls, xs, ring_r, py_r, oy_r, y_r, t_r, z_r, w_r, h_r, sent,
):
    dpi = lax.axis_index("dp")
    t = lax.axis_index("tensor")
    e, c = dpi // 2, lax.rem(dpi, 2)
    xx, yh = e // 2, lax.rem(e, 2)
    y, z = t // Z, lax.rem(t, Z)
    zdev = (dpi, y * Z + lax.rem(z + 1, Z)), (dpi, y * Z + lax.rem(z + Z - 1, Z))
    ydev = (dpi, (1 - y) * Z + z)
    w = xx * 2 + c
    hdev = ((xx * 2 + 1 - yh) * 2 + c, t)

    def ring(d):
        return zdev[d]

    def ring2(d):
        return (dpi, y * Z + lax.rem(z + (2 if d == 0 else Z - 2), Z))

    def tdev(k):
        return (dpi, k)

    def wdev(k):
        return ((k // 2 * 2 + yh) * 2 + lax.rem(k, 2), t)

    def order(j):
        far = 4 - (j + 1) // 2
        return lax.rem(z + (1 - 2 * lax.rem(j + 1, 2)) * far + Z, Z)

    def loop(n, body, first=0):
        def step(i, carry):
            body(i)
            return carry

        lax.fori_loop(first, n, step, 0)

    def both(far, body):
        if far in (0, 4):
            body(lax.rem(z + far, Z))
        else:
            loop(2, lambda i: body(lax.rem(z + far + i * (Z - 2 * far), Z)))

    def on(core, body):
        pl.when(c == core)(body)

    def local(src, dst, i):
        return pltpu.make_async_copy(src, dst, ld.at[i])

    l_u, l_d = local(u_hbm, uv, 0), local(d_hbm, dv, 1)
    l_h, l_g, l_w = local(h_hbm, hv, 2), local(gain_hbm, gv, 3), local(w_hbm, wv, 4)

    def aload(j):
        k = order(j)
        return pltpu.make_async_copy(a_hbm.at[:, k], av.at[:, k], ls.at[j])


    def xload(j):
        k = order(j)
        return pltpu.make_async_copy(x_hbm.at[:, k], xv.at[:, k], xs.at[j])

    barrier = pltpu.get_barrier_semaphore()

    def hello(dev):
        pl.semaphore_signal(barrier, inc=1, device_id=dev, device_id_type=MESH)

    hello(hdev)
    loop(T - 1, lambda i: hello(tdev(lax.rem(t + 1 + i, T))))
    l_u.start()
    loop(Z, lambda j: aload(j).start())
    l_d.start()
    loop(E - 1, lambda i: hello(wdev(lax.rem(w + 1 + i, E))))
    loop(Z, lambda j: xload(j).start())
    l_h.start()
    l_g.start()
    l_w.start()

    b_rs = ShortRingReduce(lambda k, h: bm.at[k, h], br, sent.at[0], ring_r.at[0], z, ring, ring2)
    b_ag = PairRingGather(bag, sent.at[1], sent.at[27], ring_r.at[1], z, ring)
    p_rs = RingReduce(lambda k, h: pm.at[k, h], pr, sent.at[2], ring_r.at[2], z, ring)
    p_ag = RingGather(pag, sent.at[3], ring_r.at[3], z, ring, ring2)
    o_rs = RingReduce(lambda k, h: om.at[y * Z + k, h], orr, sent.at[4], ring_r.at[4], z, ring)

    def p_y(j):
        k = order(j)
        return rc(pt.at[k], py.at[k], sent.at[5], py_r.at[j], ydev)

    def o_y(j):
        k = order(j)
        return rc(om.at[(1 - y) * Z + k], oy.at[k], sent.at[6], oy_r.at[j], ydev)

    b_y = rc(bag.at[z, 0], bag.at[z, 1], sent.at[7], y_r.at[0], ydev)

    def b_far(far):
        k = lax.rem(z + far, Z)
        return rc(bag.at[k, 0], bag.at[k, 1], sent.at[25 + far], y_r.at[far - 1], ydev)

    q0_y = rc(q0.at[1], q0y, sent.at[8], y_r.at[1], ydev)

    def p_add(j):
        p_y(j).wait_recv()
        k = order(j)
        pm[k] += py[k]

    def o_add(j):
        o_y(j).wait_recv()
        k = order(j)
        om[y * Z + k] += oy[k]

    def t_copy(n, ref, k):
        return rc(ref, ref, sent.at[9 + n], t_r.at[n], tdev(k))

    def t_send(n, ref):
        loop(T - 1, lambda i: t_copy(n, ref, lax.rem(t + 1 + i, T)).start())

    def t_all(n, some):
        return t_copy(n, some, lax.rem(t + 1, T))

    def z_copy(n, src, dst, k, side=0):
        return rc(src, dst, sent.at[11 + n], z_r.at[n], tdev((y + side - 2 * y * side) * Z + k))

    def z_others(body):
        loop(Z - 1, lambda i: body(lax.rem(z + 1 + i, Z)))

    def z_gather(n, arr):
        z_others(lambda k: z_copy(n, arr.at[z], arr.at[z], k).start())

    def z_all(n, some, side=0):
        return z_copy(n, some, some, lax.rem(z + 1, Z), side)

    def w_copy(n, src, dst, k):
        return rc(src, dst, sent.at[16 + n], w_r.at[n], wdev(k))

    def w_others(body):
        loop(E - 1, lambda i: body(lax.rem(w + 1 + i, E)))

    def w_all(n, some):
        return w_copy(n, some, some, lax.rem(w + 1, E))

    def h_copy(n, src, dst):
        return rc(src, dst, sent.at[21 + n], h_r.at[n], hdev)

    l_u.wait()
    ub[...] = uv[...].astype(BF16)
    blank = jnp.zeros((64, 128), BF16)

    def back(j):
        aload(j).wait()
        k = order(j)
        u1 = jnp.concatenate([ub[...], blank], axis=0)
        u2 = jnp.concatenate([blank, ub[...]], axis=0)
        v = dot_nt(av[0, k], u1) + dot_nt(av[1, k], u2)
        bm[k] = v.reshape(2, CH // 2, 128)

    back(0)
    pl.semaphore_wait(barrier, T - 1 + E - 1 + 1)
    for d in range(2):
        b_rs.antipode(d).start()
    loop(3, back, 1)
    b_rs.begin(True)
    b_rs.begin(False)

    l_d.wait()
    dd = dv[...]
    db[...] = jnp.where(y == 0, dd, swap(dd)).astype(BF16)

    def project(j):
        k = order(j)
        xload(j).wait()
        pa = dot(xv[0, k], db[...])
        pb = dot(xv[1, k], db[...])
        low = low_lanes(CH)
        pm[k] = jnp.where(low, pa, swap(pb)).reshape(2, CH // 2, 128)
        pt[k] = jnp.where(low, swap(pa), pb).reshape(2, CH // 2, 128)

    def project_send(j):
        project(j)
        p_y(j).start()

    loop(4, project_send)
    loop(Z, back, 3)

    l_h.wait()
    l_g.wait()
    hf = hv[...].astype(F32)
    sq = jnp.sum(hf * hf, axis=1, keepdims=True)
    sq = jnp.transpose(jnp.broadcast_to(sq, (256, 128)))
    rows[t, 0:1] = sq[0:1, 0:128]
    rows[t, 1:2] = sq[0:1, 128:256]
    t_send(0, rows.at[t])

    loop(5, project_send, 4)
    b_rs.step(1)
    loop(6, project_send, 5)
    loop(8, project, 6)
    p_add(0)
    p_rs.begin(1)
    b_rs.step(2)
    p_add(1)
    p_add(2)
    p_rs.begin(2)
    b_rs.step(3)
    for h in range(2):
        bag[z, 0, h * 96 : (h + 1) * 96] = b_rs.result(h)
    b_ag.begin(0)
    b_y.start()
    loop(8, lambda j: p_y(j).start(), 6)
    p_rs.step(1)

    def grad(p, k):
        cot = (bag[k, p] * delta_multiplier).astype(BF16)
        v = dot_tn(cot[:, :64], xv[0, k]) + dot_tn(cot[:, 64:], xv[1, k])
        gt[p] += v.reshape(8, 8, 1024)

    gt[...] = jnp.zeros_like(gt)
    both(0, lambda k: grad(0, k))

    t_all(0, rows.at[0:15]).wait_recv()
    mean = jnp.sum(rows[...], axis=0) / EMBED_DIMENSION
    scale = lax.rsqrt(mean + 1e-05)
    for i in range(2):
        half = slice(i * 128, (i + 1) * 128)
        col = jnp.transpose(jnp.broadcast_to(scale[i : i + 1], (128, 128)))
        for n in range(8):
            sl = slice(n * 128, (n + 1) * 128)
            normed[half, sl] = (hv[half, sl].astype(F32) * col * gv[:, sl]).astype(BF16)

    def pack(v):
        return jnp.where(low_lanes(128), v[:128], v[128:]).reshape(8, 16, 128)

    def twice(v, p):
        keep = low_lanes(256) if p == 0 else jnp.logical_not(low_lanes(256))
        v = jnp.where(keep, v, 0.0)
        return v + swap(v)

    def out_pair(i):
        v = dot(normed[...], wv[:, pl.ds(pl.multiple_of(i * 256, 256), 256)])
        om[2 * i] = v[:, :128].reshape(2, 128, 128)
        om[2 * i + 1] = v[:, 128:].reshape(2, 128, 128)

    dhi, dlo = split(jnp.where(y == 0, dv[...], swap(dv[...])))
    v = dot(normed[...], dhi) + dot(normed[...], dlo)
    for side in range(2):
        q0[side] = pack(twice(v, side))
    q0_y.start()
    l_w.wait()
    loop(4, lambda i: out_pair((1 - y) * 4 + i))
    loop(2, lambda j: o_y(j).start())
    b_ag.step(0, 1)
    b_y.wait_recv()
    b_ag.begin(1)
    both(1, lambda k: grad(0, k))
    both(0, lambda k: grad(1, k))
    p_add(3)
    p_add(4)
    b_ag.step(0, 2)
    p_rs.step(2)
    both(2, lambda k: grad(0, k))
    b_ag.step(1, 1)
    loop(4, lambda i: out_pair(y * 4 + i))
    p_add(5)
    p_add(6)
    b_ag.step(0, 3)
    b_far(3).start()
    b_far(5).start()
    p_rs.step(3)
    both(3, lambda k: grad(0, k))
    both(1, lambda k: grad(1, k))
    b_ag.step(0, 4)
    b_far(4).start()
    loop(3, lambda j: o_y(j).start(), 2)
    both(4, lambda k: grad(0, k))

    def g_reduce(p):
        gr[p, w] = gt[p, w]
        w_others(lambda k: w_copy(p, gt.at[p, k], gr.at[p, w], k).start())

    def g_cross(p):
        w_all(p, gr.at[p, 0:7]).wait_recv()
        gh[p, 0] = jnp.sum(gr[p], axis=0)
        h_copy(p, gh.at[p, 0], gh.at[p, 1]).start()

    def g_gather(p):
        h_copy(p, gh.at[p, 0], gh.at[p, 1]).wait_recv()
        gf[p, w] = gh[p, 0] + gh[p, 1]
        w_others(lambda k: w_copy(2 + p, gf.at[p, w], gf.at[p, w], k).start())

    def g_all(p):
        return w_all(2 + p, gf.at[p, 0:7])

    def up_grad(k):
        pc = (pag[k].reshape(CH, 128) * delta_multiplier).astype(BF16)
        va = dot_tn(pc, av[0, k])
        vb = dot_tn(pc, av[1, k])
        gu[...] += (va[:64] + vb[64:]).reshape(8, 8, 128)

    def q_of(p):
        ghi, glo = split(gf[p].reshape(64, 1024))
        v = dot_nt(normed[...], jnp.concatenate([ghi, glo], axis=0))
        qg[p] = pack(v + swap(v))

    g_reduce(0)
    gu[...] = jnp.zeros_like(gu)
    p_add(7)
    p_rs.step(4)
    for h in range(2):
        pag[z, h] = p_rs.result(h)
    p_ag.begin()
    o_add(0)
    o_rs.begin(1)
    b_ag.step(1, 2)
    both(2, lambda k: grad(1, k))
    b_far(3).wait_recv()
    b_far(5).wait_recv()
    both(3, lambda k: grad(1, k))
    b_far(4).wait_recv()
    both(4, lambda k: grad(1, k))
    g_reduce(1)
    p_ag.step(1)
    g_cross(0)
    loop(4, lambda j: o_y(j).start(), 3)
    both(0, up_grad)
    both(1, up_grad)
    o_add(1)
    o_add(2)
    o_rs.begin(2)
    o_rs.step(1)
    on(1, lambda: p_ag.step(2))
    g_cross(1)
    g_gather(0)
    loop(6, lambda j: o_y(j).start(), 4)
    on(0, lambda: p_ag.step(2))
    both(2, up_grad)
    q0_y.wait_recv()
    q0[0] += q0y[...]
    q0r[z] = q0[0, z]
    z_others(lambda k: z_copy(0, q0.at[0, k], q0r.at[z], k).start())
    g_gather(1)
    loop(7, lambda j: o_y(j).start(), 6)
    o_add(3)
    o_add(4)
    on(0, lambda: o_rs.step(2))
    p_ag.step(3)
    on(1, lambda: o_rs.step(2))
    both(3, up_grad)
    both(4, up_grad)
    gur[w] = gu[...]
    w_others(lambda k: w_copy(4, gur.at[w], gur.at[w], k).start())
    loop(8, lambda j: o_y(j).start(), 7)
    z_all(0, q0r.at[0:7]).wait_recv()
    q0a[z] = jnp.sum(q0r[...], axis=0)
    z_gather(1, q0a)
    g_all(0).wait_recv()
    q_of(0)
    qgr[0, z] = qg[0, z]
    z_others(lambda k: z_copy(3, qg.at[0, k], qgr.at[0, z], k).start())
    g_all(1).wait_recv()
    q_of(1)
    loop(Z, lambda i: z_copy(4, qg.at[1, lax.rem(z + i, Z)], qgr.at[1, z], lax.rem(z + i, Z), 1).start())
    o_add(5)
    o_add(6)
    o_rs.step(3)
    w_all(4, gur.at[0:7]).wait_recv()
    guh[0] = jnp.sum(gur[...], axis=0)
    gu_h = h_copy(2, guh.at[0], guh.at[1])
    gu_h.start()
    g2 = jnp.sum(gf[...] * gf[...], axis=(0, 1))
    tile = g2[:, 0:128]
    for i in range(1, 8):
        tile = tile + g2[:, i * 128 : (i + 1) * 128]
    gu_h.wait_recv()
    guf[...] = guh[0] + guh[1]
    norms[t] = jnp.sum(tile + jnp.sum(guf[...] * guf[...], axis=0), axis=0, keepdims=True)
    t_send(1, norms.at[t])
    z_all(3, qgr.at[0, 0:7]).wait_recv()
    z_all(4, qgr.at[1], 1).wait_recv()
    qga[z] = jnp.sum(qgr[0], axis=0) + jnp.sum(qgr[1], axis=0)
    z_gather(2, qga)
    o_add(7)
    o_rs.step(4)
    for h in range(2):
        base[h] = o_rs.result(h)
    t_all(1, norms.at[0:15]).wait_recv()
    total = jnp.sum(jnp.sum(norms[...], axis=0), keepdims=True)
    factor = jnp.minimum(1.0, clip_limit / (jnp.sqrt(total) + 1e-06))
    up = uv[...] - learning_rate * factor * guf[...].reshape(64, 128)
    zero = jnp.zeros_like(up)
    z_all(1, q0a.at[0:7]).wait_recv()
    z_all(2, qga.at[0:7]).wait_recv()
    q = q0a[...].reshape(128, 128) - learning_rate * factor * qga[...].reshape(128, 128)
    for h in range(2):
        wide = jnp.concatenate([up, zero] if h == 0 else [zero, up], axis=0)
        v = jnp.dot(q, wide, precision=lax.Precision.HIGHEST, preferred_element_type=F32)
        o_ref[:, h * 128 : (h + 1) * 128] = jnp.transpose(base[h] + delta_multiplier * v)

    for exchange in (b_rs, b_ag, p_rs, p_ag, o_rs):
        exchange.drain()
    rc(py, py, sent.at[5], py_r.at[0], ydev).wait_send()
    rc(oy, oy, sent.at[6], oy_r.at[0], ydev).wait_send()
    b_y.wait_send()
    for far in (3, 4, 5):
        b_far(far).wait_send()
    q0_y.wait_send()
    z_all(0, q0r.at[0:7]).wait_send()
    t_all(0, rows.at[0:15]).wait_send()
    t_all(1, norms.at[0:15]).wait_send()
    z_all(1, q0a.at[0:7]).wait_send()
    z_all(2, qga.at[0:7]).wait_send()
    z_all(3, qgr.at[0, 0:7]).wait_send()
    z_all(4, qgr.at[1], 1).wait_send()
    for p in range(2):
        w_all(p, gr.at[p, 0:7]).wait_send()
        g_all(p).wait_send()
        h_copy(p, gh.at[p, 0], gh.at[p, 1]).wait_send()
    w_all(4, gur.at[0:7]).wait_send()
    gu_h.wait_send()


def shards(x, a, w, d, u, hidden, gain):
    V = pltpu.VMEM
    dma = pltpu.SemaphoreType.DMA
    part = (8, 2, 96, 128)
    scratch = [
        V((2, 8, 192, 1024), BF16), V((2, 8, 192, 128), BF16), V((1024, 2048), BF16), V((1024, 128), F32),
        V((64, 128), F32), V((256, 1024), BF16), V((1, 1024), F32), V((1024, 128), BF16), V((64, 128), BF16),
        V(part, F32), V((14, 96, 128), F32), V((8, 2, 192, 128), F32),
        V(part, F32), V(part, F32), V(part, F32), V((14, 96, 128), F32), V(part, F32),
        V((16, 2, 128, 128), F32), V((8, 2, 128, 128), F32), V((14, 128, 128), F32),
        V((2, 8, 8, 1024), F32), V((2, 8, 8, 1024), F32), V((2, 2, 8, 1024), F32), V((2, 8, 8, 1024), F32),
        V((8, 8, 128), F32), V((8, 8, 8, 128), F32), V((2, 8, 8, 128), F32), V((8, 8, 128), F32),
        V((16, 2, 128), F32), V((16, 1, 128), F32), V((256, 1024), BF16), V((2, 128, 128), F32),
        V((2, 8, 16, 128), F32), V((8, 16, 128), F32), V((8, 16, 128), F32), V((8, 16, 128), F32),
        V((2, 8, 16, 128), F32), V((2, 8, 16, 128), F32), V((8, 16, 128), F32),
        dma((5,)), dma((8,)), dma((8,)), dma((5, 14)), dma((8,)), dma((8,)), dma((5,)),
        dma((2,)), dma((5,)), dma((5,)), dma((3,)), dma((31,)),
    ]
    return pl.pallas_call(
        kernel,
        out_shape=jax.ShapeDtypeStruct((128, 256), F32),
        in_specs=[pl.BlockSpec(memory_space=pl.ANY)] * 7,
        out_specs=pl.BlockSpec(memory_space=pltpu.VMEM),
        scratch_shapes=scratch,
        compiler_params=pltpu.CompilerParams(
            collective_id=0, has_side_effects=True, vmem_limit_bytes=56 << 20
        ),
    )(x.reshape(2, 8, CH, 1024), a.reshape(2, 8, CH, 128), w, d, u, hidden, gain.reshape(1, 1024))


def solution(mesh):
    placed = (
        P("dp", "tensor"),
        P("dp", "tensor"),
        P("tensor", None),
        P("tensor", None),
        P(None, "tensor"),
        P("dp", "tensor"),
        P("tensor"),
    )
    return jax.shard_map(
        shards, mesh=mesh, in_specs=placed, out_specs=P("tensor", "dp"), check_vma=False
    )
```

```python
import functools

import jax
import jax.numpy as jnp
from jax import lax
from jax.experimental import pallas as pl
from jax.experimental.pallas import tpu as pltpu
from jax.sharding import PartitionSpec as P

MESH = pl.DeviceIdType.MESH
F32 = jnp.float32
BF16 = jnp.bfloat16

EMBED_DIMENSION = 16384
delta_multiplier = 2.0
learning_rate = 4.0
clip_limit = 1.0

Z = 8
T = 16
E = 8
CH = 192


def rc(src, dst, ss, rs, dev):
    return pltpu.make_async_remote_copy(
        src_ref=src, dst_ref=dst, send_sem=ss, recv_sem=rs, device_id=dev, device_id_type=MESH
    )


def low_lanes(rows):
    return lax.broadcasted_iota(jnp.int32, (rows, 128), 1) < 64


def swap(v):
    return pltpu.roll(v, 64, 1)


def dot(a, b):
    return jnp.dot(a, b, preferred_element_type=F32)


def dot_nt(a, b):
    return lax.dot_general(a, b, (((1,), (1,)), ((), ())), preferred_element_type=F32)


def dot_tn(a, b):
    return lax.dot_general(a, b, (((0,), (0,)), ((), ())), preferred_element_type=F32)


def split(v):
    hi = v.astype(BF16)
    return hi, (v - hi.astype(F32)).astype(BF16)


class RingReduce:
    def __init__(self, own, buf, ss, rs, z, dev):
        self.own, self.buf, self.ss, self.rs, self.z, self.dev = own, buf, ss, rs, z, dev

    def chunk(self, d, far):
        return lax.rem(self.z + (far if d == 0 else Z - far), Z)

    def slot(self, d, h, s):
        return d * 7 + (s - 1 if d == h else 4 + s - 2)

    def copy(self, d, h, s):
        first = 1 if d == h else 2
        if s == first:
            src = self.own(self.chunk(d, 5 - s), h)
        else:
            src = self.buf.at[self.slot(d, h, s - 1)]
        i = self.slot(d, h, s)
        return rc(src, self.buf.at[i], self.ss, self.rs.at[i], self.dev(d))

    def begin(self, first):
        for d in range(2):
            h = d if first == 1 else 1 - d
            self.copy(d, h, first).start()

    def step(self, s):
        for same in (True, False):
            if s == 1 and not same:
                continue
            for d in range(2):
                h = d if same else 1 - d
                self.copy(d, h, s).wait_recv()
                if s < 4:
                    self.buf[self.slot(d, h, s)] += self.own(self.chunk(d, 4 - s), h)[...]
                    self.copy(d, h, s + 1).start()

    def result(self, h):
        return self.own(self.z, h)[...] + (self.buf[self.slot(0, h, 4)] + self.buf[self.slot(1, h, 4)])

    def drain(self):
        rc(self.buf, self.buf, self.ss, self.rs.at[0], self.dev(0)).wait_send()


class RingGather:
    def __init__(self, arr, ss, rs, z, dev, dev2):
        self.arr, self.ss, self.rs, self.z, self.dev, self.dev2 = arr, ss, rs, z, dev, dev2

    def copy(self, d, p, s):
        k = lax.rem(self.z + (0, Z - 1, Z - 2, Z - 2)[s - 1] if d == 0 else self.z + (0, 1, 2, 2)[s - 1], Z)
        ref = self.arr.at[k, p]
        i = d * 7 + (s - 1 if d == p else 4 + s - 1)
        return rc(ref, ref, self.ss, self.rs.at[i], (self.dev2 if s == 4 else self.dev)(d))

    def begin(self):
        for p in range(2):
            for d in range(2):
                self.copy(d, p, 1).start()

    def step(self, s):
        for same in (True, False):
            for d in range(2):
                p = d if same else 1 - d
                self.copy(d, p, s).wait_recv()
                if s == 2 and same:
                    self.copy(d, p, 4).start()
                if s < 3:
                    self.copy(d, p, s + 1).start()
        if s == 3:
            for d in range(2):
                self.copy(d, d, 4).wait_recv()

    def drain(self):
        all_sent = self.arr.at[0:7]
        rc(all_sent, all_sent, self.ss, self.rs.at[0], self.dev(0)).wait_send()


class ShortRingReduce:
    def __init__(self, own, buf, ss, rs, z, dev, dev2):
        self.own, self.buf, self.ss, self.rs, self.z, self.dev, self.dev2 = own, buf, ss, rs, z, dev, dev2

    def chunk(self, d, far):
        return lax.rem(self.z + (far if d == 0 else Z - far), Z)

    def copy(self, d, h, s):
        i = d * 7 + 2 * s - 1 + h
        src = self.own(self.chunk(d, 3), h) if s == 1 else self.buf.at[i - 2]
        return rc(src, self.buf.at[i], self.ss, self.rs.at[i], self.dev(d))

    def antipode(self, d):
        i = d * 7
        return rc(self.own(self.chunk(d, 4), d), self.buf.at[i], self.ss, self.rs.at[i], self.dev2(d))

    def begin(self, same):
        for d in range(2):
            self.copy(d, d if same else 1 - d, 1).start()

    def step(self, s):
        for same in (True, False):
            for d in range(2):
                h = d if same else 1 - d
                self.copy(d, h, s).wait_recv()
                if s == 3:
                    continue
                v = self.own(self.chunk(d, 3 - s), h)[...]
                if s == 1 and same:
                    self.antipode(d).wait_recv()
                    v = v + self.buf[d * 7]
                self.buf[d * 7 + 2 * s - 1 + h] += v
                self.copy(d, h, s + 1).start()

    def result(self, h):
        return self.own(self.z, h)[...] + (self.buf[5 + h] + self.buf[12 + h])

    def drain(self):
        rc(self.buf, self.buf, self.ss, self.rs.at[0], self.dev(0)).wait_send()


class PairRingGather:
    def __init__(self, arr, ss, ss4, rs, z, dev):
        self.arr, self.ss, self.ss4, self.rs, self.z, self.dev = arr, ss, ss4, rs, z, dev

    def copy(self, d, p, s):
        k = lax.rem(self.z + (Z - s + 1 if d == 0 else s - 1), Z)
        ref = self.arr.at[k, p, d * 96 : d * 96 + 96] if s == 4 else self.arr.at[k, p]
        return rc(ref, ref, self.ss4 if s == 4 else self.ss, self.rs.at[d * 6 + p * 4 + s - 1], self.dev(d))

    def begin(self, p):
        for d in range(2):
            self.copy(d, p, 1).start()

    def step(self, p, s):
        for d in range(2):
            self.copy(d, p, s).wait_recv()
            if s < (4, 2)[p]:
                self.copy(d, p, s + 1).start()

    def drain(self):
        for ref, ss in ((self.arr.at[0:5], self.ss), (self.arr.at[0, 0], self.ss4)):
            rc(ref, ref, ss, self.rs.at[0], self.dev(0)).wait_send()


def kernel(
    x_hbm, a_hbm, w_hbm, d_hbm, u_hbm, h_hbm, gain_hbm, o_ref,
    xv, av, wv, dv, uv, hv, gv, db, ub,
    bm, br, bag, pm, pt, py, pr, pag, om, oy, orr,
    gt, gr, gh, gf, gu, gur, guh, guf, rows, norms, normed, base,
    q0, q0y, q0r, q0a, qg, qgr, qga,
    ld, ls, xs, ring_r, py_r, oy_r, y_r, t_r, z_r, w_r, h_r, sent,
):
    dpi = lax.axis_index("dp")
    t = lax.axis_index("tensor")
    e, c = dpi // 2, lax.rem(dpi, 2)
    xx, yh = e // 2, lax.rem(e, 2)
    y, z = t // Z, lax.rem(t, Z)
    zdev = (dpi, y * Z + lax.rem(z + 1, Z)), (dpi, y * Z + lax.rem(z + Z - 1, Z))
    ydev = (dpi, (1 - y) * Z + z)
    w = xx * 2 + c
    hdev = ((xx * 2 + 1 - yh) * 2 + c, t)

    def ring(d):
        return zdev[d]

    def ring2(d):
        return (dpi, y * Z + lax.rem(z + (2 if d == 0 else Z - 2), Z))

    def tdev(k):
        return (dpi, k)

    def wdev(k):
        return ((k // 2 * 2 + yh) * 2 + lax.rem(k, 2), t)

    def order(j):
        far = 4 - (j + 1) // 2
        return lax.rem(z + (1 - 2 * lax.rem(j + 1, 2)) * far + Z, Z)

    def loop(n, body, first=0):
        def step(i, carry):
            body(i)
            return carry

        lax.fori_loop(first, n, step, 0)

    def both(far, body):
        if far in (0, 4):
            body(lax.rem(z + far, Z))
        else:
            loop(2, lambda i: body(lax.rem(z + far + i * (Z - 2 * far), Z)))

    def on(core, body):
        pl.when(c == core)(body)

    def local(src, dst, i):
        return pltpu.make_async_copy(src, dst, ld.at[i])

    l_u, l_d = local(u_hbm, uv, 0), local(d_hbm, dv, 1)
    l_h, l_g, l_w = local(h_hbm, hv, 2), local(gain_hbm, gv, 3), local(w_hbm, wv, 4)

    def aload(j):
        k = order(j)
        return pltpu.make_async_copy(a_hbm.at[:, k], av.at[:, k], ls.at[j])


    def xload(j):
        k = order(j)
        return pltpu.make_async_copy(x_hbm.at[:, k], xv.at[:, k], xs.at[j])

    barrier = pltpu.get_barrier_semaphore()

    def hello(dev):
        pl.semaphore_signal(barrier, inc=1, device_id=dev, device_id_type=MESH)

    hello(hdev)
    loop(T - 1, lambda i: hello(tdev(lax.rem(t + 1 + i, T))))
    l_u.start()
    loop(Z, lambda j: aload(j).start())
    l_d.start()
    loop(E - 1, lambda i: hello(wdev(lax.rem(w + 1 + i, E))))
    loop(Z, lambda j: xload(j).start())
    l_h.start()
    l_g.start()
    l_w.start()

    b_rs = ShortRingReduce(lambda k, h: bm.at[k, h], br, sent.at[0], ring_r.at[0], z, ring, ring2)
    b_ag = PairRingGather(bag, sent.at[1], sent.at[27], ring_r.at[1], z, ring)
    p_rs = RingReduce(lambda k, h: pm.at[k, h], pr, sent.at[2], ring_r.at[2], z, ring)
    p_ag = RingGather(pag, sent.at[3], ring_r.at[3], z, ring, ring2)
    o_rs = RingReduce(lambda k, h: om.at[y * Z + k, h], orr, sent.at[4], ring_r.at[4], z, ring)

    def p_y(j):
        k = order(j)
        return rc(pt.at[k], py.at[k], sent.at[5], py_r.at[j], ydev)

    def o_y(j):
        k = order(j)
        return rc(om.at[(1 - y) * Z + k], oy.at[k], sent.at[6], oy_r.at[j], ydev)

    b_y = rc(bag.at[z, 0], bag.at[z, 1], sent.at[7], y_r.at[0], ydev)

    def b_far(far):
        k = lax.rem(z + far, Z)
        return rc(bag.at[k, 0], bag.at[k, 1], sent.at[25 + far], y_r.at[far - 1], ydev)

    q0_y = rc(q0.at[1], q0y, sent.at[8], y_r.at[1], ydev)

    def p_add(j):
        p_y(j).wait_recv()
        k = order(j)
        pm[k] += py[k]

    def o_add(j):
        o_y(j).wait_recv()
        k = order(j)
        om[y * Z + k] += oy[k]

    def t_copy(n, ref, k):
        return rc(ref, ref, sent.at[9 + n], t_r.at[n], tdev(k))

    def t_send(n, ref):
        loop(T - 1, lambda i: t_copy(n, ref, lax.rem(t + 1 + i, T)).start())

    def t_all(n, some):
        return t_copy(n, some, lax.rem(t + 1, T))

    def z_copy(n, src, dst, k, side=0):
        return rc(src, dst, sent.at[11 + n], z_r.at[n], tdev((y + side - 2 * y * side) * Z + k))

    def z_others(body):
        loop(Z - 1, lambda i: body(lax.rem(z + 1 + i, Z)))

    def z_gather(n, arr):
        z_others(lambda k: z_copy(n, arr.at[z], arr.at[z], k).start())

    def z_all(n, some, side=0):
        return z_copy(n, some, some, lax.rem(z + 1, Z), side)

    def w_copy(n, src, dst, k):
        return rc(src, dst, sent.at[16 + n], w_r.at[n], wdev(k))

    def w_others(body):
        loop(E - 1, lambda i: body(lax.rem(w + 1 + i, E)))

    def w_all(n, some):
        return w_copy(n, some, some, lax.rem(w + 1, E))

    def h_copy(n, src, dst):
        return rc(src, dst, sent.at[21 + n], h_r.at[n], hdev)

    l_u.wait()
    ub[...] = uv[...].astype(BF16)
    blank = jnp.zeros((64, 128), BF16)

    def back(j):
        aload(j).wait()
        k = order(j)
        u1 = jnp.concatenate([ub[...], blank], axis=0)
        u2 = jnp.concatenate([blank, ub[...]], axis=0)
        v = dot_nt(av[0, k], u1) + dot_nt(av[1, k], u2)
        bm[k] = v.reshape(2, CH // 2, 128)

    back(0)
    pl.semaphore_wait(barrier, T - 1 + E - 1 + 1)
    for d in range(2):
        b_rs.antipode(d).start()
    loop(3, back, 1)
    b_rs.begin(True)
    b_rs.begin(False)

    l_d.wait()
    dd = dv[...]
    db[...] = jnp.where(y == 0, dd, swap(dd)).astype(BF16)

    def project(j):
        k = order(j)
        xload(j).wait()
        pa = dot(xv[0, k], db[...])
        pb = dot(xv[1, k], db[...])
        low = low_lanes(CH)
        pm[k] = jnp.where(low, pa, swap(pb)).reshape(2, CH // 2, 128)
        pt[k] = jnp.where(low, swap(pa), pb).reshape(2, CH // 2, 128)

    def project_send(j):
        project(j)
        p_y(j).start()

    loop(4, project_send)
    loop(Z, back, 3)

    l_h.wait()
    l_g.wait()
    hf = hv[...].astype(F32)
    sq = jnp.sum(hf * hf, axis=1, keepdims=True)
    sq = jnp.transpose(jnp.broadcast_to(sq, (256, 128)))
    rows[t, 0:1] = sq[0:1, 0:128]
    rows[t, 1:2] = sq[0:1, 128:256]
    t_send(0, rows.at[t])

    loop(5, project_send, 4)
    b_rs.step(1)
    loop(6, project_send, 5)
    loop(8, project, 6)
    p_add(0)
    p_rs.begin(1)
    b_rs.step(2)
    p_add(1)
    p_add(2)
    p_rs.begin(2)
    b_rs.step(3)
    for h in range(2):
        bag[z, 0, h * 96 : (h + 1) * 96] = b_rs.result(h)
    b_ag.begin(0)
    b_y.start()
    loop(8, lambda j: p_y(j).start(), 6)
    p_rs.step(1)

    def grad(p, k):
        cot = (bag[k, p] * delta_multiplier).astype(BF16)
        v = dot_tn(cot[:, :64], xv[0, k]) + dot_tn(cot[:, 64:], xv[1, k])
        gt[p] += v.reshape(8, 8, 1024)

    gt[...] = jnp.zeros_like(gt)
    both(0, lambda k: grad(0, k))

    t_all(0, rows.at[0:15]).wait_recv()
    mean = jnp.sum(rows[...], axis=0) / EMBED_DIMENSION
    scale = lax.rsqrt(mean + 1e-05)
    for i in range(2):
        half = slice(i * 128, (i + 1) * 128)
        col = jnp.transpose(jnp.broadcast_to(scale[i : i + 1], (128, 128)))
        for n in range(8):
            sl = slice(n * 128, (n + 1) * 128)
            normed[half, sl] = (hv[half, sl].astype(F32) * col * gv[:, sl]).astype(BF16)

    def pack(v):
        return jnp.where(low_lanes(128), v[:128], v[128:]).reshape(8, 16, 128)

    def twice(v, p):
        keep = low_lanes(256) if p == 0 else jnp.logical_not(low_lanes(256))
        v = jnp.where(keep, v, 0.0)
        return v + swap(v)

    def out_pair(i):
        v = dot(normed[...], wv[:, pl.ds(pl.multiple_of(i * 256, 256), 256)])
        om[2 * i] = v[:, :128].reshape(2, 128, 128)
        om[2 * i + 1] = v[:, 128:].reshape(2, 128, 128)

    dhi, dlo = split(jnp.where(y == 0, dv[...], swap(dv[...])))
    v = dot(normed[...], dhi) + dot(normed[...], dlo)
    for side in range(2):
        q0[side] = pack(twice(v, side))
    q0_y.start()
    l_w.wait()
    loop(4, lambda i: out_pair((1 - y) * 4 + i))
    loop(2, lambda j: o_y(j).start())
    b_ag.step(0, 1)
    b_y.wait_recv()
    b_ag.begin(1)
    both(1, lambda k: grad(0, k))
    both(0, lambda k: grad(1, k))
    p_add(3)
    p_add(4)
    b_ag.step(0, 2)
    p_rs.step(2)
    both(2, lambda k: grad(0, k))
    b_ag.step(1, 1)
    loop(4, lambda i: out_pair(y * 4 + i))
    p_add(5)
    p_add(6)
    b_ag.step(0, 3)
    b_far(3).start()
    b_far(5).start()
    p_rs.step(3)
    both(3, lambda k: grad(0, k))
    both(1, lambda k: grad(1, k))
    b_ag.step(0, 4)
    b_far(4).start()
    loop(3, lambda j: o_y(j).start(), 2)
    both(4, lambda k: grad(0, k))

    def g_reduce(p):
        gr[p, w] = gt[p, w]
        w_others(lambda k: w_copy(p, gt.at[p, k], gr.at[p, w], k).start())

    def g_cross(p):
        w_all(p, gr.at[p, 0:7]).wait_recv()
        gh[p, 0] = jnp.sum(gr[p], axis=0)
        h_copy(p, gh.at[p, 0], gh.at[p, 1]).start()

    def g_gather(p):
        h_copy(p, gh.at[p, 0], gh.at[p, 1]).wait_recv()
        gf[p, w] = gh[p, 0] + gh[p, 1]
        w_others(lambda k: w_copy(2 + p, gf.at[p, w], gf.at[p, w], k).start())

    def g_all(p):
        return w_all(2 + p, gf.at[p, 0:7])

    def up_grad(k):
        pc = (pag[k].reshape(CH, 128) * delta_multiplier).astype(BF16)
        va = dot_tn(pc, av[0, k])
        vb = dot_tn(pc, av[1, k])
        gu[...] += (va[:64] + vb[64:]).reshape(8, 8, 128)

    def q_of(p):
        ghi, glo = split(gf[p].reshape(64, 1024))
        v = dot_nt(normed[...], jnp.concatenate([ghi, glo], axis=0))
        qg[p] = pack(v + swap(v))

    g_reduce(0)
    gu[...] = jnp.zeros_like(gu)
    p_add(7)
    p_rs.step(4)
    for h in range(2):
        pag[z, h] = p_rs.result(h)
    p_ag.begin()
    o_add(0)
    o_rs.begin(1)
    b_ag.step(1, 2)
    both(2, lambda k: grad(1, k))
    b_far(3).wait_recv()
    b_far(5).wait_recv()
    both(3, lambda k: grad(1, k))
    b_far(4).wait_recv()
    both(4, lambda k: grad(1, k))
    g_reduce(1)
    p_ag.step(1)
    g_cross(0)
    loop(4, lambda j: o_y(j).start(), 3)
    both(0, up_grad)
    both(1, up_grad)
    o_add(1)
    o_add(2)

    def more():
        o_rs.begin(2)
        o_rs.step(1)

    on(1, more)
    on(1, lambda: p_ag.step(2))
    g_cross(1)
    g_gather(0)
    loop(6, lambda j: o_y(j).start(), 4)
    on(0, lambda: p_ag.step(2))
    on(0, more)
    both(2, up_grad)
    q0_y.wait_recv()
    q0[0] += q0y[...]
    q0r[z] = q0[0, z]
    z_others(lambda k: z_copy(0, q0.at[0, k], q0r.at[z], k).start())
    g_gather(1)
    loop(7, lambda j: o_y(j).start(), 6)

    def q_own():
        g_all(0).wait_recv()
        q_of(0)
        qgr[0, z] = qg[0, z]
        z_others(lambda k: z_copy(3, qg.at[0, k], qgr.at[0, z], k).start())

    on(0, q_own)
    p_ag.step(3)
    o_add(3)
    o_add(4)
    on(1, lambda: o_rs.step(2))
    both(3, up_grad)
    both(4, up_grad)
    gur[w] = gu[...]
    w_others(lambda k: w_copy(4, gur.at[w], gur.at[w], k).start())
    on(0, lambda: o_rs.step(2))
    on(1, q_own)
    g_all(1).wait_recv()
    q_of(1)
    loop(Z, lambda i: z_copy(4, qg.at[1, lax.rem(z + i, Z)], qgr.at[1, z], lax.rem(z + i, Z), 1).start())
    z_all(0, q0r.at[0:7]).wait_recv()
    q0a[z] = jnp.sum(q0r[...], axis=0)
    z_gather(1, q0a)
    w_all(4, gur.at[0:7]).wait_recv()
    guh[0] = jnp.sum(gur[...], axis=0)
    gu_h = h_copy(2, guh.at[0], guh.at[1])
    gu_h.start()
    o_y(7).start()
    o_add(5)
    o_add(6)
    o_rs.step(3)
    g2 = jnp.sum(gf[...] * gf[...], axis=(0, 1))
    tile = g2[:, 0:128]
    for i in range(1, 8):
        tile = tile + g2[:, i * 128 : (i + 1) * 128]
    gu_h.wait_recv()
    guf[...] = guh[0] + guh[1]
    norms[t] = jnp.sum(tile + jnp.sum(guf[...] * guf[...], axis=0), axis=0, keepdims=True)
    t_send(1, norms.at[t])
    z_all(3, qgr.at[0, 0:7]).wait_recv()
    z_all(4, qgr.at[1], 1).wait_recv()
    qga[z] = jnp.sum(qgr[0], axis=0) + jnp.sum(qgr[1], axis=0)
    z_gather(2, qga)
    o_add(7)
    o_rs.step(4)
    for h in range(2):
        base[h] = o_rs.result(h)
    t_all(1, norms.at[0:15]).wait_recv()
    total = jnp.sum(jnp.sum(norms[...], axis=0), keepdims=True)
    factor = jnp.minimum(1.0, clip_limit / (jnp.sqrt(total) + 1e-06))
    up = uv[...] - learning_rate * factor * guf[...].reshape(64, 128)
    zero = jnp.zeros_like(up)
    z_all(1, q0a.at[0:7]).wait_recv()
    z_all(2, qga.at[0:7]).wait_recv()
    q = q0a[...].reshape(128, 128) - learning_rate * factor * qga[...].reshape(128, 128)
    for h in range(2):
        wide = jnp.concatenate([up, zero] if h == 0 else [zero, up], axis=0)
        v = jnp.dot(q, wide, precision=lax.Precision.HIGHEST, preferred_element_type=F32)
        o_ref[:, h * 128 : (h + 1) * 128] = jnp.transpose(base[h] + delta_multiplier * v)

    for exchange in (b_rs, b_ag, p_rs, p_ag, o_rs):
        exchange.drain()
    rc(py, py, sent.at[5], py_r.at[0], ydev).wait_send()
    rc(oy, oy, sent.at[6], oy_r.at[0], ydev).wait_send()
    b_y.wait_send()
    for far in (3, 4, 5):
        b_far(far).wait_send()
    q0_y.wait_send()
    z_all(0, q0r.at[0:7]).wait_send()
    t_all(0, rows.at[0:15]).wait_send()
    t_all(1, norms.at[0:15]).wait_send()
    z_all(1, q0a.at[0:7]).wait_send()
    z_all(2, qga.at[0:7]).wait_send()
    z_all(3, qgr.at[0, 0:7]).wait_send()
    z_all(4, qgr.at[1], 1).wait_send()
    for p in range(2):
        w_all(p, gr.at[p, 0:7]).wait_send()
        g_all(p).wait_send()
        h_copy(p, gh.at[p, 0], gh.at[p, 1]).wait_send()
    w_all(4, gur.at[0:7]).wait_send()
    gu_h.wait_send()


def shards(x, a, w, d, u, hidden, gain):
    V = pltpu.VMEM
    dma = pltpu.SemaphoreType.DMA
    part = (8, 2, 96, 128)
    scratch = [
        V((2, 8, 192, 1024), BF16), V((2, 8, 192, 128), BF16), V((1024, 2048), BF16), V((1024, 128), F32),
        V((64, 128), F32), V((256, 1024), BF16), V((1, 1024), F32), V((1024, 128), BF16), V((64, 128), BF16),
        V(part, F32), V((14, 96, 128), F32), V((8, 2, 192, 128), F32),
        V(part, F32), V(part, F32), V(part, F32), V((14, 96, 128), F32), V(part, F32),
        V((16, 2, 128, 128), F32), V((8, 2, 128, 128), F32), V((14, 128, 128), F32),
        V((2, 8, 8, 1024), F32), V((2, 8, 8, 1024), F32), V((2, 2, 8, 1024), F32), V((2, 8, 8, 1024), F32),
        V((8, 8, 128), F32), V((8, 8, 8, 128), F32), V((2, 8, 8, 128), F32), V((8, 8, 128), F32),
        V((16, 2, 128), F32), V((16, 1, 128), F32), V((256, 1024), BF16), V((2, 128, 128), F32),
        V((2, 8, 16, 128), F32), V((8, 16, 128), F32), V((8, 16, 128), F32), V((8, 16, 128), F32),
        V((2, 8, 16, 128), F32), V((2, 8, 16, 128), F32), V((8, 16, 128), F32),
        dma((5,)), dma((8,)), dma((8,)), dma((5, 14)), dma((8,)), dma((8,)), dma((5,)),
        dma((2,)), dma((5,)), dma((5,)), dma((3,)), dma((31,)),
    ]
    return pl.pallas_call(
        kernel,
        out_shape=jax.ShapeDtypeStruct((128, 256), F32),
        in_specs=[pl.BlockSpec(memory_space=pl.ANY)] * 7,
        out_specs=pl.BlockSpec(memory_space=pltpu.VMEM),
        scratch_shapes=scratch,
        compiler_params=pltpu.CompilerParams(
            collective_id=0, has_side_effects=True, vmem_limit_bytes=56 << 20
        ),
    )(x.reshape(2, 8, CH, 1024), a.reshape(2, 8, CH, 128), w, d, u, hidden, gain.reshape(1, 1024))


def solution(mesh):
    placed = (
        P("dp", "tensor"),
        P("dp", "tensor"),
        P("tensor", None),
        P("tensor", None),
        P(None, "tensor"),
        P("dp", "tensor"),
        P("tensor"),
    )
    return jax.shard_map(
        shards, mesh=mesh, in_specs=placed, out_specs=P("tensor", "dp"), check_vma=False
    )
```

```python
import functools

import jax
import jax.numpy as jnp
from jax import lax
from jax.experimental import pallas as pl
from jax.experimental.pallas import tpu as pltpu
from jax.sharding import PartitionSpec as P

MESH = pl.DeviceIdType.MESH
F32 = jnp.float32
BF16 = jnp.bfloat16

EMBED_DIMENSION = 16384
delta_multiplier = 2.0
learning_rate = 4.0
clip_limit = 1.0

Z = 8
T = 16
E = 8
CH = 192


def rc(src, dst, ss, rs, dev):
    return pltpu.make_async_remote_copy(
        src_ref=src, dst_ref=dst, send_sem=ss, recv_sem=rs, device_id=dev, device_id_type=MESH
    )


def low_lanes(rows):
    return lax.broadcasted_iota(jnp.int32, (rows, 128), 1) < 64


def swap(v):
    return pltpu.roll(v, 64, 1)


def dot(a, b):
    return jnp.dot(a, b, preferred_element_type=F32)


def dot_nt(a, b):
    return lax.dot_general(a, b, (((1,), (1,)), ((), ())), preferred_element_type=F32)


def dot_tn(a, b):
    return lax.dot_general(a, b, (((0,), (0,)), ((), ())), preferred_element_type=F32)


def split(v):
    hi = v.astype(BF16)
    return hi, (v - hi.astype(F32)).astype(BF16)


class RingReduce:
    def __init__(self, own, buf, ss, rs, z, dev):
        self.own, self.buf, self.ss, self.rs, self.z, self.dev = own, buf, ss, rs, z, dev

    def chunk(self, d, far):
        return lax.rem(self.z + (far if d == 0 else Z - far), Z)

    def slot(self, d, h, s):
        return d * 7 + (s - 1 if d == h else 4 + s - 2)

    def copy(self, d, h, s):
        first = 1 if d == h else 2
        if s == first:
            src = self.own(self.chunk(d, 5 - s), h)
        else:
            src = self.buf.at[self.slot(d, h, s - 1)]
        i = self.slot(d, h, s)
        return rc(src, self.buf.at[i], self.ss, self.rs.at[i], self.dev(d))

    def begin(self, first):
        for d in range(2):
            h = d if first == 1 else 1 - d
            self.copy(d, h, first).start()

    def step(self, s):
        for same in (True, False):
            if s == 1 and not same:
                continue
            for d in range(2):
                h = d if same else 1 - d
                self.copy(d, h, s).wait_recv()
                if s < 4:
                    self.buf[self.slot(d, h, s)] += self.own(self.chunk(d, 4 - s), h)[...]
                    self.copy(d, h, s + 1).start()

    def result(self, h):
        return self.own(self.z, h)[...] + (self.buf[self.slot(0, h, 4)] + self.buf[self.slot(1, h, 4)])

    def drain(self):
        rc(self.buf, self.buf, self.ss, self.rs.at[0], self.dev(0)).wait_send()


class RingGather:
    def __init__(self, arr, ss, rs, z, dev, dev2):
        self.arr, self.ss, self.rs, self.z, self.dev, self.dev2 = arr, ss, rs, z, dev, dev2

    def copy(self, d, p, s):
        k = lax.rem(self.z + (0, Z - 1, Z - 2, Z - 2)[s - 1] if d == 0 else self.z + (0, 1, 2, 2)[s - 1], Z)
        ref = self.arr.at[k, p]
        i = d * 7 + (s - 1 if d == p else 4 + s - 1)
        return rc(ref, ref, self.ss, self.rs.at[i], (self.dev2 if s == 4 else self.dev)(d))

    def begin(self):
        for p in range(2):
            for d in range(2):
                self.copy(d, p, 1).start()

    def step(self, s):
        for same in (True, False):
            for d in range(2):
                p = d if same else 1 - d
                self.copy(d, p, s).wait_recv()
                if s == 2 and same:
                    self.copy(d, p, 4).start()
                if s < 3:
                    self.copy(d, p, s + 1).start()

    def last(self):
        for d in range(2):
            self.copy(d, d, 4).wait_recv()

    def drain(self):
        all_sent = self.arr.at[0:7]
        rc(all_sent, all_sent, self.ss, self.rs.at[0], self.dev(0)).wait_send()


class ShortRingReduce:
    def __init__(self, own, buf, ss, rs, z, dev, dev2):
        self.own, self.buf, self.ss, self.rs, self.z, self.dev, self.dev2 = own, buf, ss, rs, z, dev, dev2

    def chunk(self, d, far):
        return lax.rem(self.z + (far if d == 0 else Z - far), Z)

    def copy(self, d, h, s):
        i = d * 7 + 2 * s - 1 + h
        src = self.own(self.chunk(d, 3), h) if s == 1 else self.buf.at[i - 2]
        return rc(src, self.buf.at[i], self.ss, self.rs.at[i], self.dev(d))

    def antipode(self, d):
        i = d * 7
        return rc(self.own(self.chunk(d, 4), d), self.buf.at[i], self.ss, self.rs.at[i], self.dev2(d))

    def begin(self, same):
        for d in range(2):
            self.copy(d, d if same else 1 - d, 1).start()

    def step(self, s):
        for same in (True, False):
            for d in range(2):
                h = d if same else 1 - d
                self.copy(d, h, s).wait_recv()
                if s == 3:
                    continue
                v = self.own(self.chunk(d, 3 - s), h)[...]
                if s == 1 and same:
                    self.antipode(d).wait_recv()
                    v = v + self.buf[d * 7]
                self.buf[d * 7 + 2 * s - 1 + h] += v
                self.copy(d, h, s + 1).start()

    def result(self, h):
        return self.own(self.z, h)[...] + (self.buf[5 + h] + self.buf[12 + h])

    def drain(self):
        rc(self.buf, self.buf, self.ss, self.rs.at[0], self.dev(0)).wait_send()


class PairRingGather:
    def __init__(self, arr, ss, ss4, rs, z, dev):
        self.arr, self.ss, self.ss4, self.rs, self.z, self.dev = arr, ss, ss4, rs, z, dev

    def copy(self, d, p, s):
        k = lax.rem(self.z + (Z - s + 1 if d == 0 else s - 1), Z)
        ref = self.arr.at[k, p, d * 96 : d * 96 + 96] if s == 4 else self.arr.at[k, p]
        return rc(ref, ref, self.ss4 if s == 4 else self.ss, self.rs.at[d * 6 + p * 4 + s - 1], self.dev(d))

    def begin(self, p):
        for d in range(2):
            self.copy(d, p, 1).start()

    def step(self, p, s):
        for d in range(2):
            self.copy(d, p, s).wait_recv()
            if s < (4, 2)[p]:
                self.copy(d, p, s + 1).start()

    def drain(self):
        for ref, ss in ((self.arr.at[0:5], self.ss), (self.arr.at[0, 0], self.ss4)):
            rc(ref, ref, ss, self.rs.at[0], self.dev(0)).wait_send()


def kernel(
    x_hbm, a_hbm, w_hbm, d_hbm, u_hbm, h_hbm, gain_hbm, o_ref,
    xv, av, wv, dv, uv, hv, gv, db, ub,
    bm, br, bag, pm, pt, py, pr, pag, om, oy, orr,
    gt, gr, gh, gf, gu, gur, guh, guf, rows, norms, normed, base,
    q0, q0y, q0r, q0a, qg, qgr, qga,
    ld, ls, xs, ring_r, py_r, oy_r, y_r, t_r, z_r, w_r, h_r, sent,
):
    dpi = lax.axis_index("dp")
    t = lax.axis_index("tensor")
    e, c = dpi // 2, lax.rem(dpi, 2)
    xx, yh = e // 2, lax.rem(e, 2)
    y, z = t // Z, lax.rem(t, Z)
    zdev = (dpi, y * Z + lax.rem(z + 1, Z)), (dpi, y * Z + lax.rem(z + Z - 1, Z))
    ydev = (dpi, (1 - y) * Z + z)
    w = xx * 2 + c
    hdev = ((xx * 2 + 1 - yh) * 2 + c, t)

    def ring(d):
        return zdev[d]

    def ring2(d):
        return (dpi, y * Z + lax.rem(z + (2 if d == 0 else Z - 2), Z))

    def tdev(k):
        return (dpi, k)

    def wdev(k):
        return ((k // 2 * 2 + yh) * 2 + lax.rem(k, 2), t)

    def order(j):
        far = 4 - (j + 1) // 2
        return lax.rem(z + (1 - 2 * lax.rem(j + 1, 2)) * far + Z, Z)

    def loop(n, body, first=0):
        def step(i, carry):
            body(i)
            return carry

        lax.fori_loop(first, n, step, 0)

    def both(far, body):
        if far in (0, 4):
            body(lax.rem(z + far, Z))
        else:
            loop(2, lambda i: body(lax.rem(z + far + i * (Z - 2 * far), Z)))

    def on(core, body):
        pl.when(c == core)(body)

    def local(src, dst, i):
        return pltpu.make_async_copy(src, dst, ld.at[i])

    l_u, l_d = local(u_hbm, uv, 0), local(d_hbm, dv, 1)
    l_h, l_g, l_w = local(h_hbm, hv, 2), local(gain_hbm, gv, 3), local(w_hbm, wv, 4)

    def aload(j):
        k = order(j)
        return pltpu.make_async_copy(a_hbm.at[:, k], av.at[:, k], ls.at[jnp.minimum(j, 1)])


    def xload(j):
        k = order(j)
        return pltpu.make_async_copy(x_hbm.at[:, k], xv.at[:, k], xs.at[j])

    barrier = pltpu.get_barrier_semaphore()

    def hello(dev):
        pl.semaphore_signal(barrier, inc=1, device_id=dev, device_id_type=MESH)

    hello(hdev)
    loop(T - 1, lambda i: hello(tdev(lax.rem(t + 1 + i, T))))
    l_u.start()
    loop(Z, lambda j: aload(j).start())
    l_d.start()
    loop(E - 1, lambda i: hello(wdev(lax.rem(w + 1 + i, E))))
    loop(Z, lambda j: xload(j).start())
    l_h.start()
    l_g.start()
    l_w.start()

    b_rs = ShortRingReduce(lambda k, h: bm.at[k, h], br, sent.at[0], ring_r.at[0], z, ring, ring2)
    b_ag = PairRingGather(bag, sent.at[1], sent.at[27], ring_r.at[1], z, ring)
    p_rs = RingReduce(lambda k, h: pm.at[k, h], pr, sent.at[2], ring_r.at[2], z, ring)
    p_ag = RingGather(pag, sent.at[3], ring_r.at[3], z, ring, ring2)
    o_rs = RingReduce(lambda k, h: om.at[y * Z + k, h], orr, sent.at[4], ring_r.at[4], z, ring)

    def p_y(j):
        k = order(j)
        return rc(pt.at[k], py.at[k], sent.at[5], py_r.at[j], ydev)

    def o_y(j):
        k = order(j)
        return rc(om.at[(1 - y) * Z + k], oy.at[k], sent.at[6], oy_r.at[j], ydev)

    b_y = rc(bag.at[z, 0], bag.at[z, 1], sent.at[7], y_r.at[0], ydev)

    def b_far(far):
        k = lax.rem(z + far, Z)
        return rc(bag.at[k, 0], bag.at[k, 1], sent.at[25 + far], y_r.at[far - 1], ydev)

    q0_y = rc(q0.at[1], q0y, sent.at[8], y_r.at[1], ydev)

    def p_add(j):
        p_y(j).wait_recv()
        k = order(j)
        pm[k] += py[k]

    def o_add(j):
        o_y(j).wait_recv()
        k = order(j)
        om[y * Z + k] += oy[k]

    def t_copy(n, ref, k):
        return rc(ref, ref, sent.at[9 + n], t_r.at[n], tdev(k))

    def t_send(n, ref):
        loop(T - 1, lambda i: t_copy(n, ref, lax.rem(t + 1 + i, T)).start())

    def t_all(n, some):
        return t_copy(n, some, lax.rem(t + 1, T))

    def z_copy(n, src, dst, k, side=0):
        return rc(src, dst, sent.at[11 + n], z_r.at[n], tdev((y + side - 2 * y * side) * Z + k))

    def z_others(body):
        loop(Z - 1, lambda i: body(lax.rem(z + 1 + i, Z)))

    def z_gather(n, arr):
        z_others(lambda k: z_copy(n, arr.at[z], arr.at[z], k).start())

    def z_all(n, some, side=0):
        return z_copy(n, some, some, lax.rem(z + 1, Z), side)

    def w_copy(n, src, dst, k):
        return rc(src, dst, sent.at[16 + n], w_r.at[n], wdev(k))

    def w_others(body):
        loop(E - 1, lambda i: body(lax.rem(w + 1 + i, E)))

    def w_all(n, some):
        return w_copy(n, some, some, lax.rem(w + 1, E))

    def h_copy(n, src, dst):
        return rc(src, dst, sent.at[21 + n], h_r.at[n], hdev)

    l_u.wait()
    ub[...] = uv[...].astype(BF16)
    blank = jnp.zeros((64, 128), BF16)

    def back(j):
        k = order(j)
        u1 = jnp.concatenate([ub[...], blank], axis=0)
        u2 = jnp.concatenate([blank, ub[...]], axis=0)
        v = dot_nt(av[0, k], u1) + dot_nt(av[1, k], u2)
        bm[k] = v.reshape(2, CH // 2, 128)

    aload(0).wait()
    back(0)
    pltpu.make_async_copy(a_hbm.at[:, 0:7], av.at[:, 0:7], ls.at[1]).wait()
    pl.semaphore_wait(barrier, T - 1 + E - 1 + 1)
    for d in range(2):
        b_rs.antipode(d).start()
    loop(3, back, 1)
    b_rs.begin(True)
    b_rs.begin(False)

    l_d.wait()
    dd = dv[...]
    db[...] = jnp.where(y == 0, dd, swap(dd)).astype(BF16)

    def project(j):
        k = order(j)
        xload(j).wait()
        pa = dot(xv[0, k], db[...])
        pb = dot(xv[1, k], db[...])
        low = low_lanes(CH)
        pm[k] = jnp.where(low, pa, swap(pb)).reshape(2, CH // 2, 128)
        pt[k] = jnp.where(low, swap(pa), pb).reshape(2, CH // 2, 128)

    def project_send(j):
        project(j)
        p_y(j).start()

    loop(4, project_send)
    loop(Z, back, 3)

    l_h.wait()
    l_g.wait()
    hf = hv[...].astype(F32)
    sq = jnp.sum(hf * hf, axis=1, keepdims=True)
    sq = jnp.transpose(jnp.broadcast_to(sq, (256, 128)))
    rows[t, 0:1] = sq[0:1, 0:128]
    rows[t, 1:2] = sq[0:1, 128:256]
    t_send(0, rows.at[t])

    loop(5, project_send, 4)
    b_rs.step(1)
    loop(6, project_send, 5)
    loop(8, project, 6)
    p_add(0)
    p_rs.begin(1)
    b_rs.step(2)
    p_add(1)
    p_add(2)
    p_rs.begin(2)
    b_rs.step(3)
    for h in range(2):
        bag[z, 0, h * 96 : (h + 1) * 96] = b_rs.result(h)
    b_ag.begin(0)
    b_y.start()
    loop(8, lambda j: p_y(j).start(), 6)
    p_rs.step(1)

    def grad(p, k):
        cot = (bag[k, p] * delta_multiplier).astype(BF16)
        v = dot_tn(cot[:, :64], xv[0, k]) + dot_tn(cot[:, 64:], xv[1, k])
        gt[p] += v.reshape(8, 8, 1024)

    gt[...] = jnp.zeros_like(gt)
    both(0, lambda k: grad(0, k))

    t_all(0, rows.at[0:15]).wait_recv()
    mean = jnp.sum(rows[...], axis=0) / EMBED_DIMENSION
    scale = lax.rsqrt(mean + 1e-05)
    for i in range(2):
        half = slice(i * 128, (i + 1) * 128)
        col = jnp.transpose(jnp.broadcast_to(scale[i : i + 1], (128, 128)))
        for n in range(8):
            sl = slice(n * 128, (n + 1) * 128)
            normed[half, sl] = (hv[half, sl].astype(F32) * col * gv[:, sl]).astype(BF16)

    def pack(v):
        return jnp.where(low_lanes(128), v[:128], v[128:]).reshape(8, 16, 128)

    def twice(v, p):
        keep = low_lanes(256) if p == 0 else jnp.logical_not(low_lanes(256))
        v = jnp.where(keep, v, 0.0)
        return v + swap(v)

    def out_pair(i):
        v = dot(normed[...], wv[:, pl.ds(pl.multiple_of(i * 256, 256), 256)])
        om[2 * i] = v[:, :128].reshape(2, 128, 128)
        om[2 * i + 1] = v[:, 128:].reshape(2, 128, 128)

    dhi, dlo = split(jnp.where(y == 0, dv[...], swap(dv[...])))
    v = dot(normed[...], dhi) + dot(normed[...], dlo)
    for side in range(2):
        q0[side] = pack(twice(v, side))
    q0_y.start()
    l_w.wait()
    loop(4, lambda i: out_pair((1 - y) * 4 + i))
    loop(2, lambda j: o_y(j).start())
    b_ag.step(0, 1)
    b_y.wait_recv()
    b_ag.begin(1)
    both(1, lambda k: grad(0, k))
    both(0, lambda k: grad(1, k))
    p_add(3)
    p_add(4)
    b_ag.step(0, 2)
    p_rs.step(2)
    both(2, lambda k: grad(0, k))
    b_ag.step(1, 1)
    loop(4, lambda i: out_pair(y * 4 + i))
    p_add(5)
    p_add(6)
    b_ag.step(0, 3)
    b_far(3).start()
    b_far(5).start()
    p_rs.step(3)
    both(3, lambda k: grad(0, k))
    both(1, lambda k: grad(1, k))
    b_ag.step(0, 4)
    b_far(4).start()
    loop(3, lambda j: o_y(j).start(), 2)
    both(4, lambda k: grad(0, k))

    def g_reduce(p):
        gr[p, w] = gt[p, w]
        w_others(lambda k: w_copy(p, gt.at[p, k], gr.at[p, w], k).start())

    def g_cross(p):
        w_all(p, gr.at[p, 0:7]).wait_recv()
        gh[p, 0] = jnp.sum(gr[p], axis=0)
        h_copy(p, gh.at[p, 0], gh.at[p, 1]).start()

    def g_gather(p):
        h_copy(p, gh.at[p, 0], gh.at[p, 1]).wait_recv()
        gf[p, w] = gh[p, 0] + gh[p, 1]
        w_others(lambda k: w_copy(2 + p, gf.at[p, w], gf.at[p, w], k).start())

    def g_all(p):
        return w_all(2 + p, gf.at[p, 0:7])

    def up_grad(k):
        pc = (pag[k].reshape(CH, 128) * delta_multiplier).astype(BF16)
        va = dot_tn(pc, av[0, k])
        vb = dot_tn(pc, av[1, k])
        gu[...] += (va[:64] + vb[64:]).reshape(8, 8, 128)

    def q_of(p):
        ghi, glo = split(gf[p].reshape(64, 1024))
        v = dot_nt(normed[...], jnp.concatenate([ghi, glo], axis=0))
        qg[p] = pack(v + swap(v))

    g_reduce(0)
    gu[...] = jnp.zeros_like(gu)
    p_add(7)
    p_rs.step(4)
    for h in range(2):
        pag[z, h] = p_rs.result(h)
    p_ag.begin()
    o_add(0)
    o_rs.begin(1)
    b_ag.step(1, 2)
    both(2, lambda k: grad(1, k))
    b_far(3).wait_recv()
    b_far(5).wait_recv()
    both(3, lambda k: grad(1, k))
    b_far(4).wait_recv()
    both(4, lambda k: grad(1, k))
    g_reduce(1)
    p_ag.step(1)
    g_cross(0)
    loop(4, lambda j: o_y(j).start(), 3)
    both(0, up_grad)
    both(1, up_grad)
    o_add(1)
    o_add(2)

    def more():
        o_rs.begin(2)
        o_rs.step(1)

    on(1, more)
    on(1, lambda: p_ag.step(2))
    g_cross(1)
    g_gather(0)
    loop(6, lambda j: o_y(j).start(), 4)
    on(0, lambda: p_ag.step(2))
    on(0, more)
    both(2, up_grad)
    q0_y.wait_recv()
    q0[0] += q0y[...]
    q0r[z] = q0[0, z]
    z_others(lambda k: z_copy(0, q0.at[0, k], q0r.at[z], k).start())
    g_gather(1)
    loop(7, lambda j: o_y(j).start(), 6)

    def q_own():
        g_all(0).wait_recv()
        q_of(0)
        qgr[0, z] = qg[0, z]
        z_others(lambda k: z_copy(3, qg.at[0, k], qgr.at[0, z], k).start())

    on(0, q_own)
    p_ag.step(3)
    both(3, up_grad)
    p_ag.last()
    both(4, up_grad)
    o_add(3)
    o_add(4)
    on(1, lambda: o_rs.step(2))
    gur[w] = gu[...]
    w_others(lambda k: w_copy(4, gur.at[w], gur.at[w], k).start())
    on(0, lambda: o_rs.step(2))
    on(1, q_own)
    g_all(1).wait_recv()
    q_of(1)
    loop(Z, lambda i: z_copy(4, qg.at[1, lax.rem(z + i, Z)], qgr.at[1, z], lax.rem(z + i, Z), 1).start())
    w_all(4, gur.at[0:7]).wait_recv()
    guh[0] = jnp.sum(gur[...], axis=0)
    gu_h = h_copy(2, guh.at[0], guh.at[1])
    gu_h.start()
    o_y(7).start()
    z_all(0, q0r.at[0:7]).wait_recv()
    q0a[z] = jnp.sum(q0r[...], axis=0)
    z_gather(1, q0a)
    o_add(5)
    o_add(6)
    o_rs.step(3)
    g2 = jnp.sum(gf[...] * gf[...], axis=(0, 1))
    tile = g2[:, 0:128]
    for i in range(1, 8):
        tile = tile + g2[:, i * 128 : (i + 1) * 128]
    gu_h.wait_recv()
    guf[...] = guh[0] + guh[1]
    norms[t] = jnp.sum(tile + jnp.sum(guf[...] * guf[...], axis=0), axis=0, keepdims=True)
    t_send(1, norms.at[t])
    z_all(3, qgr.at[0, 0:7]).wait_recv()
    z_all(4, qgr.at[1], 1).wait_recv()
    qga[z] = jnp.sum(qgr[0], axis=0) + jnp.sum(qgr[1], axis=0)
    z_gather(2, qga)
    o_add(7)
    o_rs.step(4)
    for h in range(2):
        base[h] = o_rs.result(h)
    t_all(1, norms.at[0:15]).wait_recv()
    total = jnp.sum(jnp.sum(norms[...], axis=0), keepdims=True)
    factor = jnp.minimum(1.0, clip_limit / (jnp.sqrt(total) + 1e-06))
    up = uv[...] - learning_rate * factor * guf[...].reshape(64, 128)
    zero = jnp.zeros_like(up)
    z_all(1, q0a.at[0:7]).wait_recv()
    z_all(2, qga.at[0:7]).wait_recv()
    q = q0a[...].reshape(128, 128) - learning_rate * factor * qga[...].reshape(128, 128)
    for h in range(2):
        wide = jnp.concatenate([up, zero] if h == 0 else [zero, up], axis=0)
        v = jnp.dot(q, wide, precision=lax.Precision.HIGHEST, preferred_element_type=F32)
        o_ref[:, h * 128 : (h + 1) * 128] = jnp.transpose(base[h] + delta_multiplier * v)

    for exchange in (b_rs, b_ag, p_rs, p_ag, o_rs):
        exchange.drain()
    rc(py, py, sent.at[5], py_r.at[0], ydev).wait_send()
    rc(oy, oy, sent.at[6], oy_r.at[0], ydev).wait_send()
    b_y.wait_send()
    for far in (3, 4, 5):
        b_far(far).wait_send()
    q0_y.wait_send()
    z_all(0, q0r.at[0:7]).wait_send()
    t_all(0, rows.at[0:15]).wait_send()
    t_all(1, norms.at[0:15]).wait_send()
    z_all(1, q0a.at[0:7]).wait_send()
    z_all(2, qga.at[0:7]).wait_send()
    z_all(3, qgr.at[0, 0:7]).wait_send()
    z_all(4, qgr.at[1], 1).wait_send()
    for p in range(2):
        w_all(p, gr.at[p, 0:7]).wait_send()
        g_all(p).wait_send()
        h_copy(p, gh.at[p, 0], gh.at[p, 1]).wait_send()
    w_all(4, gur.at[0:7]).wait_send()
    gu_h.wait_send()


def shards(x, a, w, d, u, hidden, gain):
    V = pltpu.VMEM
    dma = pltpu.SemaphoreType.DMA
    part = (8, 2, 96, 128)
    scratch = [
        V((2, 8, 192, 1024), BF16), V((2, 8, 192, 128), BF16), V((1024, 2048), BF16), V((1024, 128), F32),
        V((64, 128), F32), V((256, 1024), BF16), V((1, 1024), F32), V((1024, 128), BF16), V((64, 128), BF16),
        V(part, F32), V((14, 96, 128), F32), V((8, 2, 192, 128), F32),
        V(part, F32), V(part, F32), V(part, F32), V((14, 96, 128), F32), V(part, F32),
        V((16, 2, 128, 128), F32), V((8, 2, 128, 128), F32), V((14, 128, 128), F32),
        V((2, 8, 8, 1024), F32), V((2, 8, 8, 1024), F32), V((2, 2, 8, 1024), F32), V((2, 8, 8, 1024), F32),
        V((8, 8, 128), F32), V((8, 8, 8, 128), F32), V((2, 8, 8, 128), F32), V((8, 8, 128), F32),
        V((16, 2, 128), F32), V((16, 1, 128), F32), V((256, 1024), BF16), V((2, 128, 128), F32),
        V((2, 8, 16, 128), F32), V((8, 16, 128), F32), V((8, 16, 128), F32), V((8, 16, 128), F32),
        V((2, 8, 16, 128), F32), V((2, 8, 16, 128), F32), V((8, 16, 128), F32),
        dma((5,)), dma((2,)), dma((8,)), dma((5, 14)), dma((8,)), dma((8,)), dma((5,)),
        dma((2,)), dma((5,)), dma((5,)), dma((3,)), dma((31,)),
    ]
    return pl.pallas_call(
        kernel,
        out_shape=jax.ShapeDtypeStruct((128, 256), F32),
        in_specs=[pl.BlockSpec(memory_space=pl.ANY)] * 7,
        out_specs=pl.BlockSpec(memory_space=pltpu.VMEM),
        scratch_shapes=scratch,
        compiler_params=pltpu.CompilerParams(
            collective_id=0, has_side_effects=True, vmem_limit_bytes=56 << 20
        ),
    )(x.reshape(2, 8, CH, 1024), a.reshape(2, 8, CH, 128), w, d, u, hidden, gain.reshape(1, 1024))


def solution(mesh):
    placed = (
        P("dp", "tensor"),
        P("dp", "tensor"),
        P("tensor", None),
        P("tensor", None),
        P(None, "tensor"),
        P("dp", "tensor"),
        P("tensor"),
    )
    return jax.shard_map(
        shards, mesh=mesh, in_specs=placed, out_specs=P("tensor", "dp"), check_vma=False
    )
```
